32 devices in a mesh: fsdp: 8 (over z, y), tp: 4 (over x, core).
Axes of the slice: x: 2, y: 2, z: 4, core: 2. Of those that a mesh axis runs over, the one named last changes fastest.
Arguments:
- hidden: bfloat16 [2, 576, 16384], P(None, 'fsdp', 'tp'), may hold values from -6 to 6
- queries: bfloat16 [2, 576, 16384], P(None, 'fsdp', 'tp'), may hold values from -256 to 256
- cache_keys: bfloat16 [576, 32, 1024], P('fsdp', None, 'tp'), may hold values from -6 to 6
- cache_values: bfloat16 [576, 32, 1024], P('fsdp', None, 'tp'), may hold values from -6 to 6
- new_values: bfloat16 [2, 576, 1024], P(None, 'fsdp', 'tp'), may hold values from -6 to 6
- lengths: int32 [576], P('fsdp'), may hold values from 2 to 32, as said below
- base_weight: bfloat16 [16384, 1024], P(None, 'tp'), may hold values from -0.046875 to 0.046875
- delta_values: bfloat16 [16384, 1024], P(('fsdp', 'tp')), may hold values from -4 to 4
- delta_scales: bfloat16 [128, 8], P('fsdp', 'tp'), may hold values from 0.0019989014 to 0.019897461
- block_order: int32 [128], replicated, may hold values from 0 to 127, each once
Outputs:
- attended: bfloat16 [2, 576, 16384], P(None, 'fsdp', 'tp')
- new_keys: bfloat16 [2, 576, 1024], P(None, 'fsdp', 'tp')
The draws below stay inside these ranges and needn't reach their ends.
Inputs may be any that keep to these rules, and one draw needn't show every extreme that they name: `lengths`: every row has at least two valid cached positions; some row holds 32. `block_order`: A permutation of the block rows.
All inputs are finite; a program needn't handle non-finite values.
Results may differ from the reference program's by a relative error of at most 0.0056.
Values may be sent and summed in bfloat16 or wider, within the bound.
No kernel may reach another device: no remote copies, remote signals or barrier semaphores. Data moves between devices by JAX's collectives and lax.ppermute only.
A program may use at most 128 MiB of HBM per device.

```python
import math
import jax
import jax.numpy as jnp
from jax import lax

D = 16384
HD = 128
KVH = 8
QH = 128
BLK = 128
STEPS = 2
CAP = 32
RTOT = 576
KVD = 1024
NBR = 128


def shared_keys(key):
    return jnp.clip(jax.random.normal(key, (RTOT, CAP, KVH * HD), jnp.float32), -6.0, 6.0)


def draw_cache_keys(key, part):
    keys_drawn = shared_keys(key)
    return keys_drawn.astype(jnp.bfloat16)


def draw_queries(key, part):
    key = jax.random.fold_in(key, 12)
    noise = jnp.clip(jax.random.normal(key, (STEPS, RTOT, QH * HD), jnp.float32), -6.0, 6.0)
    return noise.astype(jnp.bfloat16)


def draw_lengths(key, part):
    key = jax.random.fold_in(key, 13)
    drawn = jax.random.randint(key, (RTOT,), 2, CAP + 1, jnp.int32)
    return drawn.at[0].set(CAP)


def steps_of(rng, shape, shards, least, top_value):
    factor_of = 1.0
    for position, shards_of in shards:
        steps = jax.random.uniform(jax.random.fold_in(jax.random.fold_in(rng, 6), position), (shards_of,), jnp.float32, least / len(shards), top_value / len(shards))
        factor_of = factor_of * jnp.repeat(jnp.exp(steps), shape[position] // shards_of).reshape((-1,) + (1,) * (len(shape) - 1 - position))
    return factor_of


def gaussian(rng, dims, spread, limit, shards=(), held_as=jnp.bfloat16):
    values = jax.random.normal(rng, dims, jnp.float32) * spread
    if len(shards) > 0:
        values = steps_of(rng, dims, shards, -0.22, 0.18) * values
    return jnp.clip(values, min=-limit, max=limit).astype(held_as)


def setup_inputs(seed: int = 0) -> dict:
    seeds = jax.random.split(jax.random.key(seed), 11)
    return {
        "hidden": gaussian(seeds[0], (STEPS, RTOT, D), 1.0, 6.0, ((1, 8), (2, 4))),
        "queries": draw_queries(jax.random.fold_in(seeds[10], 71), 0),
        "cache_keys": draw_cache_keys(jax.random.fold_in(seeds[10], 71), 0),
        "cache_values": gaussian(seeds[3], (RTOT, CAP, KVD), 1.0, 6.0, ((0, 8), (2, 4))),
        "new_values": gaussian(seeds[4], (STEPS, RTOT, KVD), 1.0, 6.0, ((1, 8), (2, 4))),
        "lengths": draw_lengths(jax.random.fold_in(seeds[10], 71), 0),
        "base_weight": gaussian(seeds[6], (D, KVD), D ** -0.5, 0.046875, ((1, 4),)),
        "delta_values": gaussian(seeds[7], (D, KVD), 1.0, 4.0, ((0, 32),)),
        "delta_scales": jnp.clip(jnp.exp(math.log(0.019897461) - 2.2979944 * jax.random.uniform(seeds[8], (NBR, KVD // BLK), jnp.float32) ** steps_of(seeds[8], (NBR, KVD // BLK), ((0, 8), (1, 4)), -0.2, 0.2)), 0.0019989014, 0.019897461).astype(jnp.bfloat16),
        "block_order": jax.random.permutation(seeds[9], NBR).astype(jnp.int32),
    }


def reference(hidden, queries, cache_keys, cache_values, new_values, lengths, base_weight, delta_values, delta_scales, block_order):
    positions = jnp.arange(NBR).astype(jnp.int32)
    inverse = lax.optimization_barrier(jnp.sum(jnp.where(block_order[None, :] == positions[:, None], positions[None, :], 0), axis=1)).astype(jnp.int32)
    blocks = delta_values.reshape(NBR, BLK, KVD // BLK, BLK).astype(jnp.float32) * delta_scales.astype(jnp.float32)[:, None, :, None]
    blocks = lax.optimization_barrier(blocks.astype(jnp.bfloat16))
    delta = jnp.take(blocks, inverse, axis=0).reshape(D, KVD)
    refreshed = (base_weight.astype(jnp.float32) + delta.astype(jnp.float32)).astype(jnp.bfloat16)
    keys_full = jnp.dot(hidden.reshape(STEPS * RTOT, D), refreshed, preferred_element_type=jnp.float32)
    new_keys = keys_full.reshape(STEPS, RTOT, KVD).astype(jnp.bfloat16)
    group = QH // KVH
    factor = 1.0 / math.sqrt(HD)
    cache_mask = jnp.arange(CAP)[None, :] < lengths[:, None]
    step_mask = jnp.arange(STEPS)[None, :] <= jnp.arange(STEPS)[:, None]

    def one_head(head):
        query = lax.dynamic_slice_in_dim(queries, head * group * HD, group * HD, 2)
        query = query.reshape(STEPS, RTOT, group, HD).astype(jnp.float32)
        ckeys = lax.dynamic_slice_in_dim(cache_keys, head * HD, HD, 2).astype(jnp.float32)
        cvals = lax.dynamic_slice_in_dim(cache_values, head * HD, HD, 2).astype(jnp.float32)
        nkeys = lax.dynamic_slice_in_dim(new_keys, head * HD, HD, 2).astype(jnp.float32)
        nvals = lax.dynamic_slice_in_dim(new_values, head * HD, HD, 2).astype(jnp.float32)
        cached = jnp.einsum('srgd,rcd->srgc', query, ckeys) * factor
        fresh = jnp.einsum('srgd,urd->srgu', query, nkeys) * factor
        cached = jnp.where(cache_mask[None, :, None, :], cached, -1e+30)
        fresh = jnp.where(step_mask[:, None, None, :], fresh, -1e+30)
        joined = jnp.concatenate([cached, fresh], axis=3)
        top = lax.optimization_barrier(jnp.max(joined, axis=3, keepdims=True))
        expo = jnp.exp(joined - top)
        weights = (expo / lax.optimization_barrier(jnp.sum(expo, axis=3, keepdims=True))).astype(jnp.bfloat16).astype(jnp.float32)
        result = jnp.einsum('srgc,rcd->srgd', weights[..., :CAP], cvals)
        result = result + jnp.einsum('srgu,urd->srgd', weights[..., CAP:], nvals)
        return result.astype(jnp.bfloat16)
    stacked = lax.map(one_head, jnp.arange(KVH).astype(jnp.int32))
    attended = jnp.transpose(stacked, (1, 2, 0, 3, 4)).reshape(STEPS, RTOT, QH * HD)
    return (attended, new_keys)
```

```python
import functools
import math

import jax
import jax.numpy as jnp
from jax import lax
from jax.experimental import pallas as pl
from jax.experimental.pallas import tpu as pltpu
from jax.sharding import Mesh
from jax.sharding import PartitionSpec as P

HD = 128
KVH = 8
QH = 128
BLK = 128
GROUP = QH // KVH
RB = 8
MIB = 1024 * 1024
GRANT = 57 * MIB
CONTRACT_LAST = (((1,), (1,)), ((), ()))
CONTRACT_FIRST = (((0,), (0,)), ((), ()))


def params(held_bytes):
    return pltpu.CompilerParams(vmem_limit_bytes=min(60 * MIB, 8 * MIB + 2 * held_bytes))


def first_group(part, groups, parts):
    return part * (groups - row_count(groups, parts)) // max(parts - 1, 1)


def row_count(groups, parts):
    return -(-groups // parts)


def scatter_kernel(nx, parts, order_ref, *refs):
    pieces, (o_ref, all_ref, sems) = refs[:-3], refs[-3:]
    nf = o_ref.shape[0]
    per_t = all_ref.shape[2] // BLK
    per_f = order_ref.shape[0] // nf
    per_part = o_ref.shape[2] // BLK
    per_own = max(per_part // nx, 1)
    x = lax.axis_index("tx")
    core = lax.axis_index("core")

    def fetch(i):
        return pltpu.make_async_copy(pieces[i], all_ref.at[i], sems.at[i])

    for i in range(len(pieces)):
        fetch(i).start()
    for i in range(len(pieces)):
        fetch(i).wait()

    t_bits = per_t.bit_length() - 1
    assert per_t == 1 << t_bits and nx & (nx - 1) == 0
    for f in range(nf):
        for at in range(per_part):
            from_group = f * per_f + at
            if parts > 1:
                chip, rest = at // per_own, at % per_own
                from_group = f * per_f + chip * 2 * per_own + core * per_own + rest
            block = order_ref[from_group]
            owner = lax.shift_right_logical(block, t_bits)
            chip = (lax.shift_right_logical(owner, 1) + nx - x) & (nx - 1)
            index = chip * 2 + ((owner & 1) ^ core)
            lanes = pl.ds(pl.multiple_of((block & (per_t - 1)) * BLK, BLK), BLK)
            o_ref[f, :, at * BLK : (at + 1) * BLK] = all_ref[index, :, lanes]


def scatter(order, pieces, nf, split):
    rows, cols = pieces[0].shape
    width = len(pieces) * cols // nf // split
    return pl.pallas_call(
        functools.partial(scatter_kernel, len(pieces) // 2, split),
        out_shape=jax.ShapeDtypeStruct((nf, rows, width), jnp.bfloat16),
        in_specs=[pl.BlockSpec(memory_space=pltpu.SMEM)]
        + [pl.BlockSpec(memory_space=pl.ANY)] * len(pieces),
        out_specs=pl.BlockSpec(memory_space=pltpu.VMEM),
        scratch_shapes=[
            pltpu.VMEM((len(pieces), rows, cols), jnp.bfloat16),
            pltpu.SemaphoreType.DMA((len(pieces),)),
        ],
        compiler_params=params(4 * len(pieces) * rows * cols),
        cost_estimate=pl.CostEstimate(
            flops=0, bytes_accessed=3 * len(pieces) * rows * cols, transcendentals=0
        ),
        name="scatter_columns",
    )(order, *pieces)


def base_kernel(nx, info_ref, base_ref, *refs):
    pieces, (o_ref, held, sems) = refs[:-3], refs[-3:]
    width = pieces[0].shape[1]
    depth = held.shape[1]
    chunks = width // depth

    def fetch(n):
        row = pl.multiple_of(info_ref[n // chunks] * width + n % chunks * depth, depth)
        return pltpu.make_async_copy(base_ref.at[pl.ds(row, depth), :], held.at[n], sems.at[n])

    for n in range(held.shape[0]):
        fetch(n).start()
    total = jnp.zeros((o_ref.shape[0] * o_ref.shape[1], o_ref.shape[2]), jnp.float32)
    for n in range(held.shape[0]):
        lanes = slice(n % chunks * depth, (n % chunks + 1) * depth)
        first = n // chunks * nx
        part = jnp.concatenate(
            [pieces[first + r][:, lanes].astype(jnp.float32) for r in range(nx)], axis=0
        ).astype(jnp.bfloat16)
        fetch(n).wait()
        total = total + jnp.dot(part, held[n], preferred_element_type=jnp.float32)
    o_ref[...] = total.reshape(o_ref.shape)


def base_product(owners, pieces, base, nx):
    rows, width = pieces[0].shape
    cols = base.shape[1]
    quarters = len(pieces) // nx
    depth = min(width, 1024)
    count = quarters * width // depth
    size = nx * rows * cols
    return pl.pallas_call(
        functools.partial(base_kernel, nx),
        out_shape=jax.ShapeDtypeStruct((nx, rows, cols), jnp.float32),
        in_specs=[
            pl.BlockSpec(memory_space=pltpu.SMEM),
            pl.BlockSpec(memory_space=pl.ANY),
        ]
        + [pl.BlockSpec(memory_space=pltpu.VMEM)] * len(pieces),
        out_specs=pl.BlockSpec(memory_space=pltpu.VMEM),
        scratch_shapes=[
            pltpu.VMEM((count, depth, cols), jnp.bfloat16),
            pltpu.SemaphoreType.DMA((count,)),
        ],
        compiler_params=pltpu.CompilerParams(vmem_limit_bytes=GRANT),
        cost_estimate=pl.CostEstimate(
            flops=2 * size * width * quarters,
            bytes_accessed=2 * quarters * width * (cols + nx * rows) + 4 * size,
            transcendentals=0,
        ),
        name="base_keys",
    )(owners, base, *pieces)


def product_kernel(spread, part, step, s_ref, *refs):
    o_ref, scaled_ref = refs[-2:]
    x_ref, ws = refs[0], refs[1 : 1 + spread]
    earlier = refs[1 + spread : -2]
    nx, own, cols = ws[0].shape
    x = lax.axis_index("tx")
    core = lax.axis_index("core")
    for q in range(nx):
        total = earlier[0][q] if earlier else jnp.zeros((x_ref.shape[0], cols), jnp.float32)
        source = lax.rem(q + nx - x, nx)
        for d, w_ref in enumerate(ws):
            w = w_ref[q]
            at = 0
            if spread > 1:
                chip = lax.rem(x + d, nx)
                at = pl.multiple_of(chip * own, BLK)
                first = (chip * 2 + lax.bitwise_xor(core, part)) * (own // BLK)
                for b in range(own // BLK):
                    rows = slice(b * BLK, (b + 1) * BLK)
                    for c in range(cols // BLK):
                        lanes = slice(c * BLK, (c + 1) * BLK)
                        values = w_ref[q, rows, lanes].astype(jnp.float32)
                        values = values * s_ref[source, first + b, c]
                        scaled_ref[q, d, rows, lanes] = values.astype(jnp.bfloat16)
                w = scaled_ref[q, d]
            total = total + jnp.dot(
                x_ref[:, pl.ds(at, own)], w, preferred_element_type=jnp.float32
            )
        if step == "last":
            nf, _, rows, _ = o_ref.shape
            o_ref[:, q] = total.reshape(nf, rows, cols).astype(jnp.bfloat16)
        else:
            o_ref[q] = total


def product(scales, x, ws, nf, part=0, earlier=None, last=True):
    total, depth = x.shape
    nx, own, cols = ws[0].shape
    rows = total // nf
    made = nx * total * cols
    read = total * depth + len(ws) * ws[0].size
    before = [] if earlier is None else [earlier]
    out = jax.ShapeDtypeStruct((nx, total, cols), jnp.float32)
    if last:
        out = jax.ShapeDtypeStruct((nf, nx, rows, cols), jnp.bfloat16)
    return pl.pallas_call(
        functools.partial(product_kernel, len(ws), part, "last" if last else "first"),
        out_shape=out,
        in_specs=[pl.BlockSpec(memory_space=pltpu.SMEM)]
        + [pl.BlockSpec(memory_space=pltpu.VMEM)] * (1 + len(ws) + len(before)),
        out_specs=pl.BlockSpec(memory_space=pltpu.VMEM),
        scratch_shapes=[pltpu.VMEM((nx, len(ws), own, cols), jnp.bfloat16)],
        compiler_params=params(4 * read + 8 * made),
        cost_estimate=pl.CostEstimate(
            flops=2 * made * depth,
            bytes_accessed=2 * read + 6 * made,
            transcendentals=0,
        ),
        name="partial_keys",
    )(scales, x, *ws, *before)


def cached_kernel(len_ref, q_ref, ck_ref, cv_ref, qp_ref, acc_ref, ml_ref):
    step = pl.program_id(0)
    steps, taken = q_ref.shape[:2]
    cap = ck_ref.shape[1]
    heads = ck_ref.shape[2] // HD
    many = steps * GROUP * RB
    factor = 1.0 / math.sqrt(HD)
    place = lax.broadcasted_iota(jnp.int32, (cap, many), 0)
    row = lax.rem(lax.broadcasted_iota(jnp.int32, (cap, many), 1), RB)
    chains = [(i, h) for i in range(taken) for h in range(heads)]
    scores = []
    for i, h in chains:
        lanes = slice(h * HD, (h + 1) * HD)
        q = jnp.concatenate(
            [
                q_ref[s, i, :, (h * GROUP + g) * HD : (h * GROUP + g + 1) * HD].astype(jnp.float32)
                for s in range(steps)
                for g in range(GROUP)
            ],
            axis=0,
        ).astype(jnp.bfloat16)
        qp_ref[i, h] = q
        k = ck_ref[i * RB : (i + 1) * RB, :, lanes].reshape(RB * cap, HD)
        scores.append(
            lax.dot_general(k, q, CONTRACT_LAST, preferred_element_type=jnp.float32)
        )
    weights = []
    for (i, h), sc in zip(chains, scores):
        if h == 0:
            bias = jnp.concatenate(
                [
                    jnp.where(
                        (row == r) & (place < len_ref[(step * taken + i) * RB + r]), 0.0, -1e30
                    )
                    for r in range(RB)
                ],
                axis=0,
            )
        sc = sc * factor + bias
        top = jnp.max(sc, axis=0, keepdims=True)
        expo = jnp.exp(sc - top)
        ml_ref[i, h, 0:1, :] = top
        ml_ref[i, h, 1:2, :] = jnp.sum(expo, axis=0, keepdims=True)
        weights.append(expo.astype(jnp.bfloat16))
    for (i, h), expo in zip(chains, weights):
        v = cv_ref[i * RB : (i + 1) * RB, :, h * HD : (h + 1) * HD].reshape(RB * cap, HD)
        acc_ref[i, h] = lax.dot_general(
            v, expo, CONTRACT_FIRST, preferred_element_type=jnp.float32
        )


def taken_at_once(batches):
    return 3 if batches % 3 == 0 else 1


def cached(lengths, queries, cache_keys, cache_values):
    steps, batches, _, width = queries.shape
    cap, cols = cache_keys.shape[1:]
    heads = cols // HD
    many = steps * GROUP * RB
    scores = batches * heads * many * RB * cap
    n = taken_at_once(batches)
    return pl.pallas_call(
        cached_kernel,
        grid=(batches // n,),
        out_shape=(
            jax.ShapeDtypeStruct((batches, heads, many, HD), jnp.bfloat16),
            jax.ShapeDtypeStruct((batches, heads, HD, many), jnp.float32),
            jax.ShapeDtypeStruct((batches, heads, 2, many), jnp.float32),
        ),
        in_specs=[
            pl.BlockSpec(memory_space=pltpu.SMEM),
            pl.BlockSpec((steps, n, RB, width), lambda i: (0, i, 0, 0)),
            pl.BlockSpec((n * RB, cap, cols), lambda i: (i, 0, 0)),
            pl.BlockSpec((n * RB, cap, cols), lambda i: (i, 0, 0)),
        ],
        out_specs=(
            pl.BlockSpec((n, heads, many, HD), lambda i: (i, 0, 0, 0)),
            pl.BlockSpec((n, heads, HD, many), lambda i: (i, 0, 0, 0)),
            pl.BlockSpec((n, heads, 2, many), lambda i: (i, 0, 0, 0)),
        ),
        compiler_params=pltpu.CompilerParams(vmem_limit_bytes=GRANT),
        cost_estimate=pl.CostEstimate(
            flops=4 * scores * HD,
            bytes_accessed=4 * cache_keys.size + 8 * queries.size,
            transcendentals=scores,
        ),
        name="attend_cached",
    )(lengths, queries, cache_keys, cache_values)


def merge_kernel(nx, parts_ref, near_ref, far_ref, qp_ref, acc_ref, ml_ref, nv_ref, o_ref, nk_ref, held, eye):
    step = pl.program_id(0)
    steps, batches = nk_ref.shape[0], nk_ref.shape[1]
    taken, heads = acc_ref.shape[:2]
    many = steps * GROUP * RB
    factor = 1.0 / math.sqrt(HD)

    @pl.when(step == 0)
    def _():
        me = lax.axis_index("tx")
        for x in range(nx):
            for k in range(parts_ref.shape[2] // RB):
                g = first_group(x, steps * batches, nx) + k
                rows = slice(k * RB, (k + 1) * RB)
                at = lax.rem(x + nx - me, nx)
                total = near_ref[0, g * RB : (g + 1) * RB, :] + far_ref[at, rows, :]
                for f in range(parts_ref.shape[0]):
                    total = total + parts_ref[f, x, rows, :].astype(jnp.float32)
                rounded = total.astype(jnp.bfloat16)
                nk_ref[g // batches, g % batches] = rounded
                held[g // batches, g % batches] = rounded.astype(jnp.float32)
        line = lax.broadcasted_iota(jnp.int32, (many, many), 0)
        lane = lax.broadcasted_iota(jnp.int32, (many, many), 1)
        eye[...] = jnp.where(line == lane, 1.0, 0.0).astype(jnp.bfloat16)

    key = lax.broadcasted_iota(jnp.int32, (steps * RB, many), 0)
    lane = lax.broadcasted_iota(jnp.int32, (steps * RB, many), 1)
    same_row = lax.rem(key, RB) == lax.rem(lane, RB)
    known = lax.div(key, RB) <= lax.div(lane, GROUP * RB)
    bias = jnp.where(same_row & known, 0.0, -1e30)
    chains = [(i, h) for i in range(taken) for h in range(heads)]
    scores = []
    for i, h in chains:
        lanes = slice(h * HD, (h + 1) * HD)
        keys = jnp.concatenate([held[u, step * taken + i, :, lanes] for u in range(steps)], axis=0)
        scores.append(
            lax.dot_general(
                keys.astype(jnp.bfloat16),
                qp_ref[i, h],
                CONTRACT_LAST,
                preferred_element_type=jnp.float32,
            )
        )
    added, scales = [], []
    for (i, h), sn in zip(chains, scores):
        lanes = slice(h * HD, (h + 1) * HD)
        values = jnp.concatenate(
            [nv_ref[u, i, :, lanes].astype(jnp.float32) for u in range(steps)], axis=0
        )
        sn = sn * factor + bias
        old = ml_ref[i, h, 0:1, :]
        top = jnp.maximum(old, jnp.max(sn, axis=0, keepdims=True))
        keep = jnp.exp(old - top)
        expo = jnp.exp(sn - top)
        whole = ml_ref[i, h, 1:2, :] * keep + jnp.sum(expo, axis=0, keepdims=True)
        inverse = 1.0 / whole
        scales.append(keep * inverse)
        added.append(
            lax.dot_general(
                values.astype(jnp.bfloat16),
                (expo * inverse).astype(jnp.bfloat16),
                CONTRACT_FIRST,
                preferred_element_type=jnp.float32,
            )
        )
    turned = [
        (acc_ref[i, h] * scale + more).astype(jnp.bfloat16)
        for (i, h), scale, more in zip(chains, scales, added)
    ]
    for (i, h), out in zip(chains, turned):
        out = lax.dot_general(
            eye[...], out, CONTRACT_LAST, preferred_element_type=jnp.float32
        ).astype(jnp.bfloat16)
        for s in range(steps):
            for g in range(GROUP):
                at = (s * GROUP + g) * RB
                o_ref[s, i, :, (h * GROUP + g) * HD : (h * GROUP + g + 1) * HD] = out[
                    at : at + RB
                ]


def merge(parts, near, far, packed, sums, tops, new_values):
    batches, heads, many, _ = packed.shape
    steps, _, _, cols = new_values.shape
    width = many // steps // RB * heads * HD
    n = taken_at_once(batches)
    return pl.pallas_call(
        functools.partial(merge_kernel, parts.shape[1]),
        grid=(batches // n,),
        out_shape=(
            jax.ShapeDtypeStruct((steps, batches, RB, width), jnp.bfloat16),
            jax.ShapeDtypeStruct(new_values.shape, jnp.bfloat16),
        ),
        in_specs=[
            pl.BlockSpec(parts.shape, lambda i: (0, 0, 0, 0)),
            pl.BlockSpec(near.shape, lambda i: (0, 0, 0)),
            pl.BlockSpec(far.shape, lambda i: (0, 0, 0)),
            pl.BlockSpec((n, heads, many, HD), lambda i: (i, 0, 0, 0)),
            pl.BlockSpec((n, heads, HD, many), lambda i: (i, 0, 0, 0)),
            pl.BlockSpec((n, heads, 2, many), lambda i: (i, 0, 0, 0)),
            pl.BlockSpec((steps, n, RB, cols), lambda i: (0, i, 0, 0)),
        ],
        out_specs=(
            pl.BlockSpec((steps, n, RB, width), lambda i: (0, i, 0, 0)),
            pl.BlockSpec(new_values.shape, lambda i: (0, 0, 0, 0)),
        ),
        scratch_shapes=[
            pltpu.VMEM(new_values.shape, jnp.float32),
            pltpu.VMEM((many, many), jnp.bfloat16),
        ],
        compiler_params=pltpu.CompilerParams(vmem_limit_bytes=GRANT),
        cost_estimate=pl.CostEstimate(
            flops=4 * packed.size * many,
            bytes_accessed=8 * packed.size + 4 * parts.size,
            transcendentals=packed.size // 8,
        ),
        name="attend_new",
    )(parts, near, far, packed, sums, tops, new_values)


def shift_of(nx, d):
    return [(s, (s - d) % nx) for s in range(nx)]


def part_of(array, start, size, dim):
    starts = [0] * array.ndim
    starts[dim] = start
    sizes = list(array.shape)
    sizes[dim] = size
    return lax.dynamic_slice(array, starts, sizes, allow_negative_indices=False)


def after(arrays, earlier):
    return list(lax.optimization_barrier((*arrays, earlier))[:-1])


def swap(piece):
    return lax.ppermute(piece, "core", [(0, 1), (1, 0)])


def per_device(
    nf,
    nx,
    hidden,
    queries,
    cache_keys,
    cache_values,
    new_values,
    lengths,
    base_weight,
    delta_values,
    delta_scales,
    block_order,
):
    steps, rows, width = hidden.shape
    cols = base_weight.shape[1]
    batches = rows // RB
    count = row_count(steps * batches, nx)
    x = lax.axis_index("tx")
    core = lax.axis_index("core")
    depth = 2 * nx * width // nf
    own = delta_values.shape[0]
    split = 2 if own % BLK == 0 else 1

    flat = hidden.reshape(steps * rows, width)
    slices = []
    for d in range(nx):
        start = first_group(lax.rem(x + d, nx), steps * batches, nx) * RB
        slices.append(part_of(flat, start, count * RB, 0))
    held = [[None] * nx for _ in range(nx)]
    for d in range(nx):
        came = lax.ppermute(slices[-d % nx], "tx", shift_of(nx, d)) if d else slices[0]
        held[d][0] = (came, swap(came))
    mine = scatter(block_order, [p for d in range(nx) for p in held[d][0]], nf, split)

    def to_shift(d, e):
        return [(s * 2 + c, (s - d) % nx * 2 + (c ^ e)) for s in range(nx) for c in range(2)]

    shifts = [(d, e) for d in range(nx) for e in range(2)]
    sent = []
    for e in range(2):
        to = lax.bitwise_xor(core, e)
        sent.append(
            jnp.stack([part_of(delta_values, (2 * q + to) * cols, cols, 1) for q in range(nx)])
        )
    behind = after(sent, held[-1][0][0])
    ws = [sent[0]]
    for d, e in shifts[1:]:
        ws.append(lax.ppermute((behind if d else sent)[e], ("tx", "core"), to_shift(d, e)))
    arrived = ws[1:]
    scales = [delta_scales]
    scales += [lax.ppermute(delta_scales, "tx", shift_of(nx, d)) for d in range(1, nx)]
    scales = jnp.stack(scales).astype(jnp.float32)
    if split == 1:
        by_chip = jnp.repeat(jnp.roll(scales, x, axis=0), BLK, axis=2)
        whole = jnp.zeros((nx, depth, cols), jnp.bfloat16)
        for (d, e), piece in zip(shifts, ws):
            at = (lax.rem(x + d, nx) * 2 + lax.bitwise_xor(core, e)) * own
            factor = jnp.take(by_chip, (at + jnp.arange(own)) // BLK, axis=1)
            piece = (piece.astype(jnp.float32) * factor).astype(jnp.bfloat16)
            whole = lax.dynamic_update_slice_in_dim(whole, piece, at, 1)
        ws = [whole]

    (soon,) = after([flat], mine)
    late = []
    for d in range(1, nx):
        for r in range(1, nx):
            start = first_group(lax.rem(x + (r - d) % nx, nx), steps * batches, nx) * RB
            late.append(part_of(soon, start, count * RB, 0))
            (piece,) = after(late[-1:], arrived[-1])
            came = lax.ppermute(piece, "tx", shift_of(nx, d))
            held[d][r] = (came, swap(came))

    owners = [lax.rem(x + d, nx) * 2 + lax.bitwise_xor(core, e) for d, e in shifts]
    first, then = after([jnp.stack(owners[:2]), lengths], mine)
    for piece in late:
        (first,) = after([first], piece)
    near = base_product(first, [flat, swap(soon)], base_weight, 1)
    shape = (steps, batches, RB)
    share = cached(
        then, queries.reshape(shape + queries.shape[2:]), cache_keys, cache_values
    )
    mine = lax.all_to_all(mine, "fsdp", 0, 0, tiled=True)
    xs = [mine.reshape(nf * count * RB, depth // split)]
    for earlier in (*arrived, near, share[0]):
        xs = after(xs, earlier)
    if split > 1:
        xs.append(swap(xs[0]))
        partial = product(scales, xs[0], ws[0::2], nf, 0, last=False)
        partial = product(scales, xs[1], ws[1::2], nf, 1, partial)
    else:
        partial = product(scales, xs[0], ws, nf)
    parts = lax.all_to_all(
        partial.reshape(nf * nx, count * RB, cols), ("fsdp", "tx"), 0, 0, tiled=True
    ).reshape(nf, nx, count * RB, cols)
    (rest,) = after([jnp.stack(owners[2:])], partial)
    ordered = [held[d][r][e] for d in range(1, nx) for e in range(2) for r in range(nx)]
    far = base_product(rest, ordered, base_weight, nx)
    attended, new_keys = merge(parts, near, far, *share, new_values.reshape(shape + (cols,)))
    return (attended.reshape(queries.shape), new_keys.reshape(steps, rows, cols))


def solution(mesh):
    nf, nt = mesh.shape["fsdp"], mesh.shape["tp"]
    fine = Mesh(mesh.devices.reshape(nf, nt // 2, 2), ("fsdp", "tx", "core"))
    tp = ("tx", "core")
    in_specs = (
        P(None, "fsdp", tp),
        P(None, "fsdp", tp),
        P("fsdp", None, tp),
        P("fsdp", None, tp),
        P(None, "fsdp", tp),
        P("fsdp"),
        P(None, tp),
        P(("fsdp", "tx", "core"), None),
        P("fsdp", tp),
        P(),
    )
    out_specs = (P(None, "fsdp", tp), P(None, "fsdp", tp))
    return jax.shard_map(
        functools.partial(per_device, nf, nt // 2),
        mesh=fine,
        in_specs=in_specs,
        out_specs=out_specs,
        check_vma=False,
    )
```

```python
import functools
import math

import jax
import jax.numpy as jnp
from jax import lax
from jax.experimental import pallas as pl
from jax.experimental.pallas import tpu as pltpu
from jax.sharding import Mesh
from jax.sharding import PartitionSpec as P

HD = 128
KVH = 8
QH = 128
BLK = 128
GROUP = QH // KVH
RB = 8
MIB = 1024 * 1024
GRANT = 57 * MIB
MIDDLE = 52 * MIB
BESIDE = pl.CostEstimate(flops=0, bytes_accessed=1024, transcendentals=0)
CONTRACT_LAST = (((1,), (1,)), ((), ()))
CONTRACT_FIRST = (((0,), (0,)), ((), ()))


def params(held_bytes):
    return pltpu.CompilerParams(vmem_limit_bytes=min(60 * MIB, 8 * MIB + 2 * held_bytes))


def first_group(part, groups, parts):
    return part * (groups - row_count(groups, parts)) // max(parts - 1, 1)


def row_count(groups, parts):
    return -(-groups // parts)


def scatter_kernel(nx, parts, order_ref, *refs):
    pieces, (o_ref, all_ref, sems) = refs[:-3], refs[-3:]
    nf = o_ref.shape[0]
    per_t = all_ref.shape[2] // BLK
    per_f = order_ref.shape[0] // nf
    per_part = o_ref.shape[2] // BLK
    per_own = max(per_part // nx, 1)
    x = lax.axis_index("tx")
    core = lax.axis_index("core")

    def fetch(i):
        piece = pieces[i]
        if len(piece.shape) == 3:
            piece = piece.at[x]
        return pltpu.make_async_copy(piece, all_ref.at[i], sems.at[i])

    for i in range(len(pieces)):
        fetch(i).start()
    for i in range(len(pieces)):
        fetch(i).wait()

    t_bits = per_t.bit_length() - 1
    assert per_t == 1 << t_bits and nx & (nx - 1) == 0
    for f in range(nf):
        for at in range(per_part):
            from_group = f * per_f + at
            if parts > 1:
                chip, rest = at // per_own, at % per_own
                from_group = f * per_f + chip * 2 * per_own + core * per_own + rest
            block = order_ref[from_group]
            owner = lax.shift_right_logical(block, t_bits)
            chip = (lax.shift_right_logical(owner, 1) + nx - x) & (nx - 1)
            index = chip * 2 + ((owner & 1) ^ core)
            lanes = pl.ds(pl.multiple_of((block & (per_t - 1)) * BLK, BLK), BLK)
            o_ref[f, :, at * BLK : (at + 1) * BLK] = all_ref[index, :, lanes]


def scatter(order, pieces, nf, split):
    rows, cols = pieces[-1].shape
    width = len(pieces) * cols // nf // split
    return pl.pallas_call(
        functools.partial(scatter_kernel, len(pieces) // 2, split),
        out_shape=jax.ShapeDtypeStruct((nf, rows, width), jnp.bfloat16),
        in_specs=[pl.BlockSpec(memory_space=pltpu.SMEM)]
        + [pl.BlockSpec(memory_space=pl.ANY)] * len(pieces),
        out_specs=pl.BlockSpec(memory_space=pltpu.VMEM),
        scratch_shapes=[
            pltpu.VMEM((len(pieces), rows, cols), jnp.bfloat16),
            pltpu.SemaphoreType.DMA((len(pieces),)),
        ],
        compiler_params=params(4 * len(pieces) * rows * cols),
        cost_estimate=pl.CostEstimate(
            flops=0, bytes_accessed=3 * len(pieces) * rows * cols, transcendentals=0
        ),
        name="scatter_columns",
    )(order, *pieces)


def base_kernel(plan, info_ref, base_ref, *refs):
    count = sum(len(targets) for targets in plan)
    made = 1 + max(max(targets) for targets in plan)
    pieces, outs, taken = refs[:count], refs[count : count + made], refs[count + made : -2]
    held, sems = refs[-2:]
    depth = held.shape[1]
    width = taken[0].shape[1]
    chunks = width // depth
    total = held.shape[0]

    def take(i):
        return pltpu.make_async_copy(pieces[i], taken[i], sems.at[total + i])

    def fetch(n):
        row = pl.multiple_of(info_ref[n // chunks] * width + n % chunks * depth, depth)
        return pltpu.make_async_copy(base_ref.at[pl.ds(row, depth), :], held.at[n], sems.at[n])

    firsts = [sum(len(targets) for targets in plan[:q]) for q in range(len(plan))]
    for q, targets in enumerate(plan):
        for r in range(len(targets)):
            take(firsts[q] + r).start()
        for j in range(chunks):
            fetch(q * chunks + j).start()
    sums = [jnp.zeros(o_ref.shape, jnp.float32) for o_ref in outs]
    for q, targets in enumerate(plan):
        for r in range(len(targets)):
            take(firsts[q] + r).wait()
        for j in range(chunks):
            n = q * chunks + j
            fetch(n).wait()
            for r, target in enumerate(targets):
                part = taken[firsts[q] + r][:, j * depth : (j + 1) * depth]
                sums[target] = sums[target] + jnp.dot(
                    part, held[n], preferred_element_type=jnp.float32
                )
    for o_ref, value in zip(outs, sums):
        o_ref[...] = value


def base_product(owners, plan, pieces, base, grant):
    width = pieces[0].shape[1]
    cols = base.shape[1]
    depth = min(width, 1024)
    count = len(plan) * width // depth
    rows = {}
    for target, piece in zip([t for targets in plan for t in targets], pieces):
        rows[target] = piece.shape[0]
    return pl.pallas_call(
        functools.partial(base_kernel, plan),
        out_shape=tuple(
            jax.ShapeDtypeStruct((rows[t], cols), jnp.float32) for t in range(len(rows))
        ),
        in_specs=[pl.BlockSpec(memory_space=pltpu.SMEM)]
        + [pl.BlockSpec(memory_space=pl.ANY)] * (1 + len(pieces)),
        out_specs=(pl.BlockSpec(memory_space=pltpu.VMEM),) * len(rows),
        scratch_shapes=[pltpu.VMEM(piece.shape, jnp.bfloat16) for piece in pieces]
        + [
            pltpu.VMEM((count, depth, cols), jnp.bfloat16),
            pltpu.SemaphoreType.DMA((count + len(pieces),)),
        ],
        compiler_params=pltpu.CompilerParams(vmem_limit_bytes=grant),
        cost_estimate=BESIDE,
        name="base_keys",
    )(owners, base, *pieces)


def scale_kernel(nx, shifts, *refs):
    scales, refs = refs[:nx], refs[nx:]
    pieces, outs = refs[: len(shifts)], refs[len(shifts) :]
    own, cols = pieces[0].shape[1:]
    x = lax.axis_index("tx")
    core = lax.axis_index("core")
    for (d, e), piece, o_ref in zip(shifts, pieces, outs):
        first = (lax.rem(x + d, nx) * 2 + lax.bitwise_xor(core, e)) * (own // BLK)
        for q in range(nx):
            source = lax.rem(q + nx - x, nx)
            for b in range(own // BLK):
                rows = slice(b * BLK, (b + 1) * BLK)
                for c in range(cols // BLK):
                    lanes = slice(c * BLK, (c + 1) * BLK)
                    factor = scales[0][first + b, c]
                    for n in range(1, nx):
                        factor = jnp.where(source == n, scales[n][first + b, c], factor)
                    values = piece[q, rows, lanes].astype(jnp.float32) * factor
                    o_ref[q, rows, lanes] = values.astype(jnp.bfloat16)


def scale_rows(scales, shifts, pieces):
    size = len(pieces) * pieces[0].size
    return pl.pallas_call(
        functools.partial(scale_kernel, pieces[0].shape[0], shifts),
        out_shape=tuple(jax.ShapeDtypeStruct(p.shape, jnp.bfloat16) for p in pieces),
        in_specs=[pl.BlockSpec(memory_space=pltpu.SMEM)] * len(scales)
        + [pl.BlockSpec(memory_space=pltpu.VMEM)] * len(pieces),
        out_specs=(pl.BlockSpec(memory_space=pltpu.VMEM),) * len(pieces),
        compiler_params=params(4 * size),
        cost_estimate=BESIDE,
        name="scale_rows",
    )(*scales, *pieces)


def product_kernel(spread, step, *refs):
    o_ref = refs[-1]
    x_ref, ws = refs[0], refs[1 : 1 + spread]
    earlier = refs[1 + spread : -1]
    nx, own, cols = ws[0].shape
    x = lax.axis_index("tx")
    for q in range(nx):
        total = earlier[0][q] if earlier else jnp.zeros((x_ref.shape[0], cols), jnp.float32)
        for d, w_ref in enumerate(ws):
            at = 0
            if spread > 1:
                at = pl.multiple_of(lax.rem(x + d, nx) * own, BLK)
            total = total + jnp.dot(
                x_ref[:, pl.ds(at, own)], w_ref[q], preferred_element_type=jnp.float32
            )
        if step == "last":
            nf, _, rows, _ = o_ref.shape
            o_ref[:, q] = total.reshape(nf, rows, cols).astype(jnp.bfloat16)
        else:
            o_ref[q] = total


def product(x, ws, nf, earlier=None, last=True):
    total, depth = x.shape
    nx, _, cols = ws[0].shape
    rows = total // nf
    made = nx * total * cols
    read = total * depth + len(ws) * ws[0].size
    before = [] if earlier is None else [earlier]
    out = jax.ShapeDtypeStruct((nx, total, cols), jnp.float32)
    if last:
        out = jax.ShapeDtypeStruct((nf, nx, rows, cols), jnp.bfloat16)
    return pl.pallas_call(
        functools.partial(product_kernel, len(ws), "last" if last else "first"),
        out_shape=out,
        in_specs=[pl.BlockSpec(memory_space=pltpu.VMEM)] * (1 + len(ws) + len(before)),
        out_specs=pl.BlockSpec(memory_space=pltpu.VMEM),
        compiler_params=params(2 * read + 8 * made),
        cost_estimate=pl.CostEstimate(
            flops=2 * made * depth,
            bytes_accessed=2 * read + 6 * made,
            transcendentals=0,
        ),
        name="partial_keys",
    )(x, *ws, *before)


def cached_kernel(len_ref, q_ref, ck_ref, cv_ref, qp_ref, acc_ref, ml_ref):
    step = pl.program_id(0)
    steps, taken = q_ref.shape[:2]
    cap = ck_ref.shape[1]
    heads = ck_ref.shape[2] // HD
    many = steps * GROUP * RB
    factor = 1.0 / math.sqrt(HD)
    place = lax.broadcasted_iota(jnp.int32, (cap, many), 0)
    row = lax.rem(lax.broadcasted_iota(jnp.int32, (cap, many), 1), RB)
    chains = [(i, h) for i in range(taken) for h in range(heads)]
    scores = []
    for i, h in chains:
        lanes = slice(h * HD, (h + 1) * HD)
        q = jnp.concatenate(
            [
                q_ref[s, i, :, (h * GROUP + g) * HD : (h * GROUP + g + 1) * HD].astype(jnp.float32)
                for s in range(steps)
                for g in range(GROUP)
            ],
            axis=0,
        ).astype(jnp.bfloat16)
        qp_ref[i, h] = q
        k = ck_ref[i * RB : (i + 1) * RB, :, lanes].reshape(RB * cap, HD)
        scores.append(
            lax.dot_general(k, q, CONTRACT_LAST, preferred_element_type=jnp.float32)
        )
    weights = []
    for (i, h), sc in zip(chains, scores):
        if h == 0:
            bias = jnp.concatenate(
                [
                    jnp.where(
                        (row == r) & (place < len_ref[(step * taken + i) * RB + r]), 0.0, -1e30
                    )
                    for r in range(RB)
                ],
                axis=0,
            )
        sc = sc * factor + bias
        top = jnp.max(sc, axis=0, keepdims=True)
        expo = jnp.exp(sc - top)
        ml_ref[i, h, 0:1, :] = top
        ml_ref[i, h, 1:2, :] = jnp.sum(expo, axis=0, keepdims=True)
        weights.append(expo.astype(jnp.bfloat16))
    for (i, h), expo in zip(chains, weights):
        v = cv_ref[i * RB : (i + 1) * RB, :, h * HD : (h + 1) * HD].reshape(RB * cap, HD)
        acc_ref[i, h] = lax.dot_general(
            v, expo, CONTRACT_FIRST, preferred_element_type=jnp.float32
        )


def taken_at_once(batches):
    return 3 if batches % 3 == 0 else 1


def cached(lengths, queries, cache_keys, cache_values):
    steps, batches, _, width = queries.shape
    cap, cols = cache_keys.shape[1:]
    heads = cols // HD
    many = steps * GROUP * RB
    n = taken_at_once(batches)
    return pl.pallas_call(
        cached_kernel,
        grid=(batches // n,),
        out_shape=(
            jax.ShapeDtypeStruct((batches, heads, many, HD), jnp.bfloat16),
            jax.ShapeDtypeStruct((batches, heads, HD, many), jnp.float32),
            jax.ShapeDtypeStruct((batches, heads, 2, many), jnp.float32),
        ),
        in_specs=[
            pl.BlockSpec(memory_space=pltpu.SMEM),
            pl.BlockSpec((steps, n, RB, width), lambda i: (0, i, 0, 0)),
            pl.BlockSpec((n * RB, cap, cols), lambda i: (i, 0, 0)),
            pl.BlockSpec((n * RB, cap, cols), lambda i: (i, 0, 0)),
        ],
        out_specs=(
            pl.BlockSpec((n, heads, many, HD), lambda i: (i, 0, 0, 0)),
            pl.BlockSpec((n, heads, HD, many), lambda i: (i, 0, 0, 0)),
            pl.BlockSpec((n, heads, 2, many), lambda i: (i, 0, 0, 0)),
        ),
        compiler_params=pltpu.CompilerParams(vmem_limit_bytes=MIDDLE),
        cost_estimate=BESIDE,
        name="attend_cached",
    )(lengths, queries, cache_keys, cache_values)


def merge_kernel(nx, parts_ref, near_ref, far_ref, *refs):
    late_refs, (qp_ref, acc_ref, ml_ref, nv_ref, o_ref, nk_ref, held, eye) = refs[: nx - 1], refs[nx - 1 :]
    step = pl.program_id(0)
    steps, batches = nk_ref.shape[0], nk_ref.shape[1]
    taken, heads = acc_ref.shape[:2]
    many = steps * GROUP * RB
    factor = 1.0 / math.sqrt(HD)

    @pl.when(step == 0)
    def _():
        me = lax.axis_index("tx")
        for x in range(nx):
            for k in range(parts_ref.shape[2] // RB):
                g = first_group(x, steps * batches, nx) + k
                rows = slice(k * RB, (k + 1) * RB)
                at = lax.rem(x + nx - me, nx)
                total = near_ref[g * RB : (g + 1) * RB, :]
                far = far_ref[rows, :]
                for r, late_ref in enumerate(late_refs):
                    far = jnp.where(at == r + 1, late_ref[rows, :], far)
                total = total + far
                for f in range(parts_ref.shape[0]):
                    total = total + parts_ref[f, x, rows, :].astype(jnp.float32)
                rounded = total.astype(jnp.bfloat16)
                nk_ref[g // batches, g % batches] = rounded
                held[g // batches, g % batches] = rounded.astype(jnp.float32)
        line = lax.broadcasted_iota(jnp.int32, (many, many), 0)
        lane = lax.broadcasted_iota(jnp.int32, (many, many), 1)
        eye[...] = jnp.where(line == lane, 1.0, 0.0).astype(jnp.bfloat16)

    key = lax.broadcasted_iota(jnp.int32, (steps * RB, many), 0)
    lane = lax.broadcasted_iota(jnp.int32, (steps * RB, many), 1)
    same_row = lax.rem(key, RB) == lax.rem(lane, RB)
    known = lax.div(key, RB) <= lax.div(lane, GROUP * RB)
    bias = jnp.where(same_row & known, 0.0, -1e30)
    chains = [(i, h) for i in range(taken) for h in range(heads)]
    scores = []
    for i, h in chains:
        lanes = slice(h * HD, (h + 1) * HD)
        keys = jnp.concatenate([held[u, step * taken + i, :, lanes] for u in range(steps)], axis=0)
        scores.append(
            lax.dot_general(
                keys.astype(jnp.bfloat16),
                qp_ref[i, h],
                CONTRACT_LAST,
                preferred_element_type=jnp.float32,
            )
        )
    added, scales = [], []
    for (i, h), sn in zip(chains, scores):
        lanes = slice(h * HD, (h + 1) * HD)
        values = jnp.concatenate(
            [nv_ref[u, i, :, lanes].astype(jnp.float32) for u in range(steps)], axis=0
        )
        sn = sn * factor + bias
        old = ml_ref[i, h, 0:1, :]
        top = jnp.maximum(old, jnp.max(sn, axis=0, keepdims=True))
        keep = jnp.exp(old - top)
        expo = jnp.exp(sn - top)
        whole = ml_ref[i, h, 1:2, :] * keep + jnp.sum(expo, axis=0, keepdims=True)
        inverse = 1.0 / whole
        scales.append(keep * inverse)
        added.append(
            lax.dot_general(
                values.astype(jnp.bfloat16),
                (expo * inverse).astype(jnp.bfloat16),
                CONTRACT_FIRST,
                preferred_element_type=jnp.float32,
            )
        )
    turned = [
        (acc_ref[i, h] * scale + more).astype(jnp.bfloat16)
        for (i, h), scale, more in zip(chains, scales, added)
    ]
    for (i, h), out in zip(chains, turned):
        out = lax.dot_general(
            eye[...], out, CONTRACT_LAST, preferred_element_type=jnp.float32
        ).astype(jnp.bfloat16)
        for s in range(steps):
            for g in range(GROUP):
                at = (s * GROUP + g) * RB
                o_ref[s, i, :, (h * GROUP + g) * HD : (h * GROUP + g + 1) * HD] = out[
                    at : at + RB
                ]


def merge(parts, near, far, late, packed, sums, tops, new_values):
    batches, heads, many, _ = packed.shape
    steps, _, _, cols = new_values.shape
    width = many // steps // RB * heads * HD
    n = taken_at_once(batches)
    return pl.pallas_call(
        functools.partial(merge_kernel, parts.shape[1]),
        grid=(batches // n,),
        out_shape=(
            jax.ShapeDtypeStruct((steps, batches, RB, width), jnp.bfloat16),
            jax.ShapeDtypeStruct(new_values.shape, jnp.bfloat16),
        ),
        in_specs=[
            pl.BlockSpec(parts.shape, lambda i: (0, 0, 0, 0)),
            *(pl.BlockSpec(part.shape, lambda i: (0, 0)) for part in (near, far, *late)),
            pl.BlockSpec((n, heads, many, HD), lambda i: (i, 0, 0, 0)),
            pl.BlockSpec((n, heads, HD, many), lambda i: (i, 0, 0, 0)),
            pl.BlockSpec((n, heads, 2, many), lambda i: (i, 0, 0, 0)),
            pl.BlockSpec((steps, n, RB, cols), lambda i: (0, i, 0, 0)),
        ],
        out_specs=(
            pl.BlockSpec((steps, n, RB, width), lambda i: (0, i, 0, 0)),
            pl.BlockSpec(new_values.shape, lambda i: (0, 0, 0, 0)),
        ),
        scratch_shapes=[
            pltpu.VMEM(new_values.shape, jnp.float32),
            pltpu.VMEM((many, many), jnp.bfloat16),
        ],
        compiler_params=pltpu.CompilerParams(vmem_limit_bytes=GRANT),
        cost_estimate=pl.CostEstimate(
            flops=4 * packed.size * many,
            bytes_accessed=8 * packed.size + 4 * parts.size,
            transcendentals=packed.size // 8,
        ),
        name="attend_new",
    )(parts, near, far, *late, packed, sums, tops, new_values)


def shift_of(nx, d):
    return [(s, (s - d) % nx) for s in range(nx)]


def part_of(array, start, size, dim):
    starts = [0] * array.ndim
    starts[dim] = start
    sizes = list(array.shape)
    sizes[dim] = size
    return lax.dynamic_slice(array, starts, sizes, allow_negative_indices=False)


def after(arrays, earlier):
    return list(lax.optimization_barrier((*arrays, earlier))[:-1])


def swap(piece):
    return lax.ppermute(piece, "core", [(0, 1), (1, 0)])


def per_device(
    nf,
    nx,
    hidden,
    queries,
    cache_keys,
    cache_values,
    new_values,
    lengths,
    base_weight,
    delta_values,
    delta_scales,
    block_order,
):
    steps, rows, width = hidden.shape
    cols = base_weight.shape[1]
    batches = rows // RB
    count = row_count(steps * batches, nx)
    x = lax.axis_index("tx")
    core = lax.axis_index("core")
    depth = 2 * nx * width // nf
    own = delta_values.shape[0]
    split = 2 if own % BLK == 0 else 1

    def to_shift(d, e):
        return [(s * 2 + c, (s - d) % nx * 2 + (c ^ e)) for s in range(nx) for c in range(2)]

    shifts = [(d, e) for d in range(nx) for e in range(2)]
    sent = []
    for e in range(2):
        to = lax.bitwise_xor(core, e)
        sent.append(
            jnp.stack([part_of(delta_values, (2 * q + to) * cols, cols, 1) for q in range(nx)])
        )
    scales = [delta_scales.astype(jnp.float32)]
    scales += [lax.ppermute(scales[0], "tx", shift_of(nx, d)) for d in range(1, nx)]

    flat = hidden.reshape(steps * rows, width)
    whole_rows = swap(flat)

    def rows_of(array, d):
        start = first_group(lax.rem(x + d, nx), steps * batches, nx) * RB
        return part_of(array, start, count * RB, 0)

    held = [[None] * nx for _ in range(nx)]
    for d in range(1, nx):
        came = lax.ppermute(rows_of(flat, (-d) % nx), "tx", shift_of(nx, d))
        ready = [came]
        for early in (*sent, scales[d]):
            ready = after(ready, early)
        held[d][0] = (came, swap(ready[0]))
    if nx == steps and count * RB == rows:
        pieces = [hidden, whole_rows.reshape(hidden.shape)]
    else:
        pieces = [rows_of(flat, 0), rows_of(whole_rows, 0)]
    pieces += [p for d in range(1, nx) for p in held[d][0]]
    mine = scatter(block_order, pieces, nf, split)

    behind = after(sent, held[-1][0][0])
    ws = [sent[0]]
    for d, e in shifts[1:]:
        ws.append(lax.ppermute((behind if d else sent)[e], ("tx", "core"), to_shift(d, e)))
    arrived = ws[1:]
    if split > 1:
        ws = [
            *scale_rows(scales, shifts[:2], ws[:2]),
            *scale_rows(scales, shifts[2:], ws[2:]),
        ]
    if split == 1:
        by_chip = jnp.repeat(jnp.roll(jnp.stack(scales), x, axis=0), BLK, axis=2)
        whole = jnp.zeros((nx, depth, cols), jnp.bfloat16)
        for (d, e), piece in zip(shifts, ws):
            at = (lax.rem(x + d, nx) * 2 + lax.bitwise_xor(core, e)) * own
            factor = jnp.take(by_chip, (at + jnp.arange(own)) // BLK, axis=1)
            piece = (piece.astype(jnp.float32) * factor).astype(jnp.bfloat16)
            whole = lax.dynamic_update_slice_in_dim(whole, piece, at, 1)
        ws = [whole]

    (soon,) = after([flat], mine)
    late = []
    for d in range(1, nx):
        for r in range(1, nx):
            start = first_group(lax.rem(x + (r - d) % nx, nx), steps * batches, nx) * RB
            late.append(part_of(soon, start, count * RB, 0))
            (piece,) = after(late[-1:], arrived[-1])
            came = lax.ppermute(piece, "tx", shift_of(nx, d))
            held[d][r] = (came, swap(came))

    owners = [lax.rem(x + d, nx) * 2 + lax.bitwise_xor(core, e) for d, e in shifts]
    owners = jnp.stack(owners)
    first, then = after([owners, lengths], mine)
    for piece in (*late, *ws[:1]):
        (first,) = after([first], piece)
    early = [held[d][0][e] for d in range(1, nx) for e in range(2)]
    plan = ((0,),) * 2 + ((1,),) * len(early)
    near, far = base_product(first, plan, [flat, whole_rows, *early], base_weight, MIDDLE)
    shape = (steps, batches, RB)
    share = cached(
        then, queries.reshape(shape + queries.shape[2:]), cache_keys, cache_values
    )
    mine = lax.all_to_all(mine, "fsdp", 0, 0, tiled=True)
    xs = [mine.reshape(nf * count * RB, depth // split)]
    for earlier in (*arrived, near, far, share[0]):
        xs = after(xs, earlier)
    if split > 1:
        xs.append(swap(xs[0]))
        partial = product(xs[0], ws[0::2], nf, last=False)
        partial = product(xs[1], ws[1::2], nf, partial)
    else:
        partial = product(xs[0], ws, nf)
    parts = lax.all_to_all(
        partial.reshape(nf * nx, count * RB, cols), ("fsdp", "tx"), 0, 0, tiled=True
    ).reshape(nf, nx, count * RB, cols)
    remaining = [held[d][r][e] for d in range(1, nx) for e in range(2) for r in range(1, nx)]
    plan = (tuple(range(nx - 1)),) * (2 * (nx - 1))
    late = base_product(after([owners[2:]], partial)[0], plan, remaining, base_weight, GRANT)
    attended, new_keys = merge(parts, near, far, late, *share, new_values.reshape(shape + (cols,)))
    return (attended.reshape(queries.shape), new_keys.reshape(steps, rows, cols))


def solution(mesh):
    nf, nt = mesh.shape["fsdp"], mesh.shape["tp"]
    fine = Mesh(mesh.devices.reshape(nf, nt // 2, 2), ("fsdp", "tx", "core"))
    tp = ("tx", "core")
    in_specs = (
        P(None, "fsdp", tp),
        P(None, "fsdp", tp),
        P("fsdp", None, tp),
        P("fsdp", None, tp),
        P(None, "fsdp", tp),
        P("fsdp"),
        P(None, tp),
        P(("fsdp", "tx", "core"), None),
        P("fsdp", tp),
        P(),
    )
    out_specs = (P(None, "fsdp", tp), P(None, "fsdp", tp))
    return jax.shard_map(
        functools.partial(per_device, nf, nt // 2),
        mesh=fine,
        in_specs=in_specs,
        out_specs=out_specs,
        check_vma=False,
    )
```

```python
import functools
import math

import jax
import jax.numpy as jnp
from jax import lax
from jax.experimental import pallas as pl
from jax.experimental.pallas import tpu as pltpu
from jax.sharding import Mesh
from jax.sharding import PartitionSpec as P

HD = 128
KVH = 8
QH = 128
BLK = 128
GROUP = QH // KVH
RB = 8
MIB = 1024 * 1024
GRANT = 57 * MIB
MIDDLE = 52 * MIB
LATE = 55 * MIB
BESIDE = pl.CostEstimate(flops=0, bytes_accessed=1024, transcendentals=0)
CONTRACT_LAST = (((1,), (1,)), ((), ()))
CONTRACT_FIRST = (((0,), (0,)), ((), ()))


def params(held_bytes):
    return pltpu.CompilerParams(vmem_limit_bytes=min(60 * MIB, 8 * MIB + 2 * held_bytes))


def first_group(part, groups, parts):
    return part * (groups - row_count(groups, parts)) // max(parts - 1, 1)


def row_count(groups, parts):
    return -(-groups // parts)


def scatter_kernel(nx, parts, order_ref, *refs):
    pieces, (out_ref, o_ref, all_ref, sems) = refs[:-4], refs[-4:]
    nf = o_ref.shape[0]
    per_t = all_ref.shape[2] // BLK
    per_f = order_ref.shape[0] // nf
    per_part = o_ref.shape[2] // BLK
    per_own = max(per_part // nx, 1)
    x = lax.axis_index("tx")
    core = lax.axis_index("core")

    def fetch(i):
        piece = pieces[i]
        if len(piece.shape) == 3:
            piece = piece.at[x]
        return pltpu.make_async_copy(piece, all_ref.at[i], sems.at[i])

    def send(f):
        return pltpu.make_async_copy(o_ref.at[f], out_ref.at[f], sems.at[len(pieces) + f])

    for i in range(len(pieces)):
        fetch(i).start()
    for i in range(len(pieces)):
        fetch(i).wait()

    t_bits = per_t.bit_length() - 1
    assert per_t == 1 << t_bits and nx & (nx - 1) == 0
    for f in range(nf):
        for at in range(per_part):
            from_group = f * per_f + at
            if parts > 1:
                chip, rest = at // per_own, at % per_own
                from_group = f * per_f + chip * 2 * per_own + core * per_own + rest
            block = order_ref[from_group]
            owner = lax.shift_right_logical(block, t_bits)
            chip = (lax.shift_right_logical(owner, 1) + nx - x) & (nx - 1)
            index = chip * 2 + ((owner & 1) ^ core)
            lanes = pl.ds(pl.multiple_of((block & (per_t - 1)) * BLK, BLK), BLK)
            o_ref[f, :, at * BLK : (at + 1) * BLK] = all_ref[index, :, lanes]
        send(f).start()
    for f in range(nf):
        send(f).wait()


def scatter(order, pieces, nf, split):
    rows, cols = pieces[-1].shape
    width = len(pieces) * cols // nf // split
    return pl.pallas_call(
        functools.partial(scatter_kernel, len(pieces) // 2, split),
        out_shape=jax.ShapeDtypeStruct((nf, rows, width), jnp.bfloat16),
        in_specs=[pl.BlockSpec(memory_space=pltpu.SMEM)]
        + [pl.BlockSpec(memory_space=pl.ANY)] * len(pieces),
        out_specs=pl.BlockSpec(memory_space=pl.ANY),
        scratch_shapes=[
            pltpu.VMEM((nf, rows, width), jnp.bfloat16),
            pltpu.VMEM((len(pieces), rows, cols), jnp.bfloat16),
            pltpu.SemaphoreType.DMA((len(pieces) + nf,)),
        ],
        compiler_params=params(4 * len(pieces) * rows * cols),
        cost_estimate=pl.CostEstimate(
            flops=0, bytes_accessed=3 * len(pieces) * rows * cols, transcendentals=0
        ),
        name="scatter_columns",
    )(order, *pieces)


def base_kernel(plan, info_ref, base_ref, *refs):
    count = sum(len(targets) for targets in plan)
    made = 1 + max(max(targets) for targets in plan)
    pieces, outs, taken = refs[:count], refs[count : count + made], refs[count + made : -2]
    held, sems = refs[-2:]
    depth = held.shape[1]
    width = taken[0].shape[1]
    chunks = width // depth
    total = held.shape[0]

    def take(i):
        return pltpu.make_async_copy(pieces[i], taken[i], sems.at[total + i])

    def fetch(n):
        row = pl.multiple_of(info_ref[n // chunks] * width + n % chunks * depth, depth)
        return pltpu.make_async_copy(base_ref.at[pl.ds(row, depth), :], held.at[n], sems.at[n])

    firsts = [sum(len(targets) for targets in plan[:q]) for q in range(len(plan))]
    for q, targets in enumerate(plan):
        for r in range(len(targets)):
            take(firsts[q] + r).start()
        for j in range(chunks):
            fetch(q * chunks + j).start()
    sums = [jnp.zeros(o_ref.shape, jnp.float32) for o_ref in outs]
    for q, targets in enumerate(plan):
        for r in range(len(targets)):
            take(firsts[q] + r).wait()
        for j in range(chunks):
            n = q * chunks + j
            fetch(n).wait()
            for r, target in enumerate(targets):
                part = taken[firsts[q] + r][:, j * depth : (j + 1) * depth]
                sums[target] = sums[target] + jnp.dot(
                    part, held[n], preferred_element_type=jnp.float32
                )
    for o_ref, value in zip(outs, sums):
        o_ref[...] = value


def base_product(owners, plan, pieces, base, grant):
    width = pieces[0].shape[1]
    cols = base.shape[1]
    depth = min(width, 1024)
    count = len(plan) * width // depth
    rows = {}
    for target, piece in zip([t for targets in plan for t in targets], pieces):
        rows[target] = piece.shape[0]
    return pl.pallas_call(
        functools.partial(base_kernel, plan),
        out_shape=tuple(
            jax.ShapeDtypeStruct((rows[t], cols), jnp.float32) for t in range(len(rows))
        ),
        in_specs=[pl.BlockSpec(memory_space=pltpu.SMEM)]
        + [pl.BlockSpec(memory_space=pl.ANY)] * (1 + len(pieces)),
        out_specs=(pl.BlockSpec(memory_space=pltpu.VMEM),) * len(rows),
        scratch_shapes=[pltpu.VMEM(piece.shape, jnp.bfloat16) for piece in pieces]
        + [
            pltpu.VMEM((count, depth, cols), jnp.bfloat16),
            pltpu.SemaphoreType.DMA((count + len(pieces),)),
        ],
        compiler_params=pltpu.CompilerParams(vmem_limit_bytes=grant),
        cost_estimate=BESIDE,
        name="base_keys",
    )(owners, base, *pieces)


def scale_kernel(nx, shifts, *refs):
    scales, refs = refs[:nx], refs[nx:]
    pieces, outs = refs[: len(shifts)], refs[len(shifts) :]
    own, cols = pieces[0].shape[1:]
    x = lax.axis_index("tx")
    core = lax.axis_index("core")
    for (d, e), piece, o_ref in zip(shifts, pieces, outs):
        first = (lax.rem(x + d, nx) * 2 + lax.bitwise_xor(core, e)) * (own // BLK)
        for q in range(nx):
            source = lax.rem(q + nx - x, nx)
            for b in range(own // BLK):
                rows = slice(b * BLK, (b + 1) * BLK)
                for c in range(cols // BLK):
                    lanes = slice(c * BLK, (c + 1) * BLK)
                    factor = scales[0][first + b, c]
                    for n in range(1, nx):
                        factor = jnp.where(source == n, scales[n][first + b, c], factor)
                    values = piece[q, rows, lanes].astype(jnp.float32) * factor
                    o_ref[q, rows, lanes] = values.astype(jnp.bfloat16)


def scale_rows(scales, shifts, pieces):
    size = len(pieces) * pieces[0].size
    return pl.pallas_call(
        functools.partial(scale_kernel, pieces[0].shape[0], shifts),
        out_shape=tuple(jax.ShapeDtypeStruct(p.shape, jnp.bfloat16) for p in pieces),
        in_specs=[pl.BlockSpec(memory_space=pltpu.SMEM)] * len(scales)
        + [pl.BlockSpec(memory_space=pltpu.VMEM)] * len(pieces),
        out_specs=(pl.BlockSpec(memory_space=pltpu.VMEM),) * len(pieces),
        compiler_params=params(4 * size),
        cost_estimate=BESIDE,
        name="scale_rows",
    )(*scales, *pieces)


def product_kernel(spread, step, *refs):
    o_ref = refs[-1]
    x_ref, ws = refs[0], refs[1 : 1 + spread]
    earlier = refs[1 + spread : -1]
    nx, own, cols = ws[0].shape
    x = lax.axis_index("tx")
    for q in range(nx):
        total = earlier[0][q] if earlier else jnp.zeros((x_ref.shape[0], cols), jnp.float32)
        for d, w_ref in enumerate(ws):
            at = 0
            if spread > 1:
                at = pl.multiple_of(lax.rem(x + d, nx) * own, BLK)
            total = total + jnp.dot(
                x_ref[:, pl.ds(at, own)], w_ref[q], preferred_element_type=jnp.float32
            )
        if step == "last":
            nf, _, rows, _ = o_ref.shape
            o_ref[:, q] = total.reshape(nf, rows, cols).astype(jnp.bfloat16)
        else:
            o_ref[q] = total


def product(x, ws, nf, earlier=None, last=True):
    total, depth = x.shape
    nx, _, cols = ws[0].shape
    rows = total // nf
    made = nx * total * cols
    read = total * depth + len(ws) * ws[0].size
    before = [] if earlier is None else [earlier]
    out = jax.ShapeDtypeStruct((nx, total, cols), jnp.float32)
    if last:
        out = jax.ShapeDtypeStruct((nf, nx, rows, cols), jnp.bfloat16)
    return pl.pallas_call(
        functools.partial(product_kernel, len(ws), "last" if last else "first"),
        out_shape=out,
        in_specs=[pl.BlockSpec(memory_space=pltpu.VMEM)] * (1 + len(ws) + len(before)),
        out_specs=pl.BlockSpec(memory_space=pltpu.VMEM),
        compiler_params=params(2 * read + 8 * made),
        cost_estimate=pl.CostEstimate(
            flops=2 * made * depth,
            bytes_accessed=2 * read + 6 * made,
            transcendentals=0,
        ),
        name="partial_keys",
    )(x, *ws, *before)


def cached_kernel(len_ref, q_ref, ck_ref, cv_ref, qp_ref, acc_ref, ml_ref):
    step = pl.program_id(0)
    steps, taken = q_ref.shape[:2]
    cap = ck_ref.shape[1]
    heads = ck_ref.shape[2] // HD
    many = steps * GROUP * RB
    factor = 1.0 / math.sqrt(HD)
    place = lax.broadcasted_iota(jnp.int32, (cap, many), 0)
    row = lax.rem(lax.broadcasted_iota(jnp.int32, (cap, many), 1), RB)
    chains = [(i, h) for i in range(taken) for h in range(heads)]
    scores = []
    for i, h in chains:
        lanes = slice(h * HD, (h + 1) * HD)
        q = jnp.concatenate(
            [
                q_ref[s, i, :, (h * GROUP + g) * HD : (h * GROUP + g + 1) * HD].astype(jnp.float32)
                for s in range(steps)
                for g in range(GROUP)
            ],
            axis=0,
        ).astype(jnp.bfloat16)
        qp_ref[i, h] = q
        k = ck_ref[i * RB : (i + 1) * RB, :, lanes].reshape(RB * cap, HD)
        scores.append(
            lax.dot_general(k, q, CONTRACT_LAST, preferred_element_type=jnp.float32)
        )
    weights = []
    for (i, h), sc in zip(chains, scores):
        if h == 0:
            bias = jnp.concatenate(
                [
                    jnp.where(
                        (row == r) & (place < len_ref[(step * taken + i) * RB + r]), 0.0, -1e30
                    )
                    for r in range(RB)
                ],
                axis=0,
            )
        sc = sc * factor + bias
        top = jnp.max(sc, axis=0, keepdims=True)
        expo = jnp.exp(sc - top)
        ml_ref[i, h, 0:1, :] = top
        ml_ref[i, h, 1:2, :] = jnp.sum(expo, axis=0, keepdims=True)
        weights.append(expo.astype(jnp.bfloat16))
    for (i, h), expo in zip(chains, weights):
        v = cv_ref[i * RB : (i + 1) * RB, :, h * HD : (h + 1) * HD].reshape(RB * cap, HD)
        acc_ref[i, h] = lax.dot_general(
            v, expo, CONTRACT_FIRST, preferred_element_type=jnp.float32
        )


def taken_at_once(batches):
    return 3 if batches % 3 == 0 else 1


def cached(lengths, queries, cache_keys, cache_values):
    steps, batches, _, width = queries.shape
    cap, cols = cache_keys.shape[1:]
    heads = cols // HD
    many = steps * GROUP * RB
    n = taken_at_once(batches)
    return pl.pallas_call(
        cached_kernel,
        grid=(batches // n,),
        out_shape=(
            jax.ShapeDtypeStruct((batches, heads, many, HD), jnp.bfloat16),
            jax.ShapeDtypeStruct((batches, heads, HD, many), jnp.float32),
            jax.ShapeDtypeStruct((batches, heads, 2, many), jnp.float32),
        ),
        in_specs=[
            pl.BlockSpec(memory_space=pltpu.SMEM),
            pl.BlockSpec((steps, n, RB, width), lambda i: (0, i, 0, 0)),
            pl.BlockSpec((n * RB, cap, cols), lambda i: (i, 0, 0)),
            pl.BlockSpec((n * RB, cap, cols), lambda i: (i, 0, 0)),
        ],
        out_specs=(
            pl.BlockSpec((n, heads, many, HD), lambda i: (i, 0, 0, 0)),
            pl.BlockSpec((n, heads, HD, many), lambda i: (i, 0, 0, 0)),
            pl.BlockSpec((n, heads, 2, many), lambda i: (i, 0, 0, 0)),
        ),
        compiler_params=pltpu.CompilerParams(vmem_limit_bytes=MIDDLE),
        cost_estimate=BESIDE,
        name="attend_cached",
    )(lengths, queries, cache_keys, cache_values)


def merge_kernel(nx, parts_ref, near_ref, far_ref, *refs):
    late_refs, (qp_ref, acc_ref, ml_ref, nv_ref, o_ref, nk_ref, held, eye) = refs[: nx - 1], refs[nx - 1 :]
    step = pl.program_id(0)
    steps, batches = nk_ref.shape[0], nk_ref.shape[1]
    taken, heads = acc_ref.shape[:2]
    many = steps * GROUP * RB
    factor = 1.0 / math.sqrt(HD)

    @pl.when(step == 0)
    def _():
        me = lax.axis_index("tx")
        for x in range(nx):
            for k in range(parts_ref.shape[2] // RB):
                g = first_group(x, steps * batches, nx) + k
                rows = slice(k * RB, (k + 1) * RB)
                at = lax.rem(x + nx - me, nx)
                total = near_ref[g * RB : (g + 1) * RB, :]
                far = far_ref[rows, :]
                for r, late_ref in enumerate(late_refs):
                    far = jnp.where(at == r + 1, late_ref[rows, :], far)
                total = total + far
                for f in range(parts_ref.shape[0]):
                    total = total + parts_ref[f, x, rows, :].astype(jnp.float32)
                rounded = total.astype(jnp.bfloat16)
                nk_ref[g // batches, g % batches] = rounded
                held[g // batches, g % batches] = rounded.astype(jnp.float32)
        line = lax.broadcasted_iota(jnp.int32, (many, many), 0)
        lane = lax.broadcasted_iota(jnp.int32, (many, many), 1)
        eye[...] = jnp.where(line == lane, 1.0, 0.0).astype(jnp.bfloat16)

    key = lax.broadcasted_iota(jnp.int32, (steps * RB, many), 0)
    lane = lax.broadcasted_iota(jnp.int32, (steps * RB, many), 1)
    same_row = lax.rem(key, RB) == lax.rem(lane, RB)
    known = lax.div(key, RB) <= lax.div(lane, GROUP * RB)
    bias = jnp.where(same_row & known, 0.0, -1e30)
    chains = [(i, h) for i in range(taken) for h in range(heads)]
    scores = []
    for i, h in chains:
        lanes = slice(h * HD, (h + 1) * HD)
        keys = jnp.concatenate([held[u, step * taken + i, :, lanes] for u in range(steps)], axis=0)
        scores.append(
            lax.dot_general(
                keys.astype(jnp.bfloat16),
                qp_ref[i, h],
                CONTRACT_LAST,
                preferred_element_type=jnp.float32,
            )
        )
    added, scales = [], []
    for (i, h), sn in zip(chains, scores):
        lanes = slice(h * HD, (h + 1) * HD)
        values = jnp.concatenate(
            [nv_ref[u, i, :, lanes].astype(jnp.float32) for u in range(steps)], axis=0
        )
        sn = sn * factor + bias
        old = ml_ref[i, h, 0:1, :]
        top = jnp.maximum(old, jnp.max(sn, axis=0, keepdims=True))
        keep = jnp.exp(old - top)
        expo = jnp.exp(sn - top)
        whole = ml_ref[i, h, 1:2, :] * keep + jnp.sum(expo, axis=0, keepdims=True)
        inverse = 1.0 / whole
        scales.append(keep * inverse)
        added.append(
            lax.dot_general(
                values.astype(jnp.bfloat16),
                (expo * inverse).astype(jnp.bfloat16),
                CONTRACT_FIRST,
                preferred_element_type=jnp.float32,
            )
        )
    turned = [
        (acc_ref[i, h] * scale + more).astype(jnp.bfloat16)
        for (i, h), scale, more in zip(chains, scales, added)
    ]
    for (i, h), out in zip(chains, turned):
        out = lax.dot_general(
            eye[...], out, CONTRACT_LAST, preferred_element_type=jnp.float32
        ).astype(jnp.bfloat16)
        for s in range(steps):
            for g in range(GROUP):
                at = (s * GROUP + g) * RB
                o_ref[s, i, :, (h * GROUP + g) * HD : (h * GROUP + g + 1) * HD] = out[
                    at : at + RB
                ]


def merge(parts, near, far, late, packed, sums, tops, new_values):
    batches, heads, many, _ = packed.shape
    steps, _, _, cols = new_values.shape
    width = many // steps // RB * heads * HD
    n = taken_at_once(batches)
    return pl.pallas_call(
        functools.partial(merge_kernel, parts.shape[1]),
        grid=(batches // n,),
        out_shape=(
            jax.ShapeDtypeStruct((steps, batches, RB, width), jnp.bfloat16),
            jax.ShapeDtypeStruct(new_values.shape, jnp.bfloat16),
        ),
        in_specs=[
            pl.BlockSpec(parts.shape, lambda i: (0, 0, 0, 0)),
            *(pl.BlockSpec(part.shape, lambda i: (0, 0)) for part in (near, far, *late)),
            pl.BlockSpec((n, heads, many, HD), lambda i: (i, 0, 0, 0)),
            pl.BlockSpec((n, heads, HD, many), lambda i: (i, 0, 0, 0)),
            pl.BlockSpec((n, heads, 2, many), lambda i: (i, 0, 0, 0)),
            pl.BlockSpec((steps, n, RB, cols), lambda i: (0, i, 0, 0)),
        ],
        out_specs=(
            pl.BlockSpec((steps, n, RB, width), lambda i: (0, i, 0, 0)),
            pl.BlockSpec(new_values.shape, lambda i: (0, 0, 0, 0)),
        ),
        scratch_shapes=[
            pltpu.VMEM(new_values.shape, jnp.float32),
            pltpu.VMEM((many, many), jnp.bfloat16),
        ],
        compiler_params=pltpu.CompilerParams(vmem_limit_bytes=GRANT),
        cost_estimate=pl.CostEstimate(
            flops=4 * packed.size * many,
            bytes_accessed=8 * packed.size + 4 * parts.size,
            transcendentals=packed.size // 8,
        ),
        name="attend_new",
    )(parts, near, far, *late, packed, sums, tops, new_values)


def shift_of(nx, d):
    return [(s, (s - d) % nx) for s in range(nx)]


def part_of(array, start, size, dim):
    starts = [0] * array.ndim
    starts[dim] = start
    sizes = list(array.shape)
    sizes[dim] = size
    return lax.dynamic_slice(array, starts, sizes, allow_negative_indices=False)


def after(arrays, earlier):
    return list(lax.optimization_barrier((*arrays, earlier))[:-1])


def swap(piece):
    return lax.ppermute(piece, "core", [(0, 1), (1, 0)])


def per_device(
    nf,
    nx,
    hidden,
    queries,
    cache_keys,
    cache_values,
    new_values,
    lengths,
    base_weight,
    delta_values,
    delta_scales,
    block_order,
):
    steps, rows, width = hidden.shape
    cols = base_weight.shape[1]
    batches = rows // RB
    count = row_count(steps * batches, nx)
    x = lax.axis_index("tx")
    core = lax.axis_index("core")
    depth = 2 * nx * width // nf
    own = delta_values.shape[0]
    split = 2 if own % BLK == 0 else 1

    def to_shift(d, e):
        return [(s * 2 + c, (s - d) % nx * 2 + (c ^ e)) for s in range(nx) for c in range(2)]

    shifts = [(d, e) for d in range(nx) for e in range(2)]
    sent = []
    for e in range(2):
        to = lax.bitwise_xor(core, e)
        sent.append(
            jnp.stack([part_of(delta_values, (2 * q + to) * cols, cols, 1) for q in range(nx)])
        )
    scales = [delta_scales.astype(jnp.float32)]
    scales += [lax.ppermute(scales[0], "tx", shift_of(nx, d)) for d in range(1, nx)]

    flat = hidden.reshape(steps * rows, width)
    whole_rows = swap(flat)

    def rows_of(array, d):
        start = first_group(lax.rem(x + d, nx), steps * batches, nx) * RB
        return part_of(array, start, count * RB, 0)

    held = [[None] * nx for _ in range(nx)]
    for d in range(1, nx):
        came = lax.ppermute(rows_of(flat, (-d) % nx), "tx", shift_of(nx, d))
        ready = [came]
        for early in (*sent, scales[d]):
            ready = after(ready, early)
        held[d][0] = (came, swap(ready[0]))
    if nx == steps and count * RB == rows:
        pieces = [hidden, whole_rows.reshape(hidden.shape)]
    else:
        pieces = [rows_of(flat, 0), rows_of(whole_rows, 0)]
    pieces += [p for d in range(1, nx) for p in held[d][0]]
    mine = scatter(block_order, pieces, nf, split)

    behind = after(sent, held[-1][0][0])
    ws = [sent[0]]
    for d, e in shifts[1:]:
        ws.append(lax.ppermute((behind if d else sent)[e], ("tx", "core"), to_shift(d, e)))
    arrived = ws[1:]
    if split > 1:
        ws[:2] = scale_rows(scales, shifts[:2], ws[:2])
    if split == 1:
        by_chip = jnp.repeat(jnp.roll(jnp.stack(scales), x, axis=0), BLK, axis=2)
        whole = jnp.zeros((nx, depth, cols), jnp.bfloat16)
        for (d, e), piece in zip(shifts, ws):
            at = (lax.rem(x + d, nx) * 2 + lax.bitwise_xor(core, e)) * own
            factor = jnp.take(by_chip, (at + jnp.arange(own)) // BLK, axis=1)
            piece = (piece.astype(jnp.float32) * factor).astype(jnp.bfloat16)
            whole = lax.dynamic_update_slice_in_dim(whole, piece, at, 1)
        ws = [whole]

    (soon,) = after([flat], mine)
    late = []
    for d in range(1, nx):
        for r in range(1, nx):
            start = first_group(lax.rem(x + (r - d) % nx, nx), steps * batches, nx) * RB
            late.append(part_of(soon, start, count * RB, 0))
            (piece,) = after(late[-1:], arrived[-1])
            came = lax.ppermute(piece, "tx", shift_of(nx, d))
            held[d][r] = (came, swap(came))

    owners = [lax.rem(x + d, nx) * 2 + lax.bitwise_xor(core, e) for d, e in shifts]
    owners = jnp.stack(owners)
    first, then = after([owners, lengths], mine)
    for piece in (*late, *ws[:1]):
        (first,) = after([first], piece)
    early = [held[d][0][e] for d in range(1, nx) for e in range(2)]
    plan = ((0,),) * 2 + ((1,),) * len(early)
    near, far = base_product(first, plan, [flat, whole_rows, *early], base_weight, MIDDLE)
    shape = (steps, batches, RB)
    share = cached(
        then, queries.reshape(shape + queries.shape[2:]), cache_keys, cache_values
    )
    if split > 1:
        for earlier in (near, far, share[0]):
            scales = after(scales, earlier)
        ws[2:] = scale_rows(scales, shifts[2:], ws[2:])
    mine = lax.all_to_all(mine, "fsdp", 0, 0, tiled=True)
    xs = [mine.reshape(nf * count * RB, depth // split)]
    for earlier in (*arrived[:1], *ws[-2:], near, far, share[0]):
        xs = after(xs, earlier)
    if split > 1:
        xs.append(swap(xs[0]))
        partial = product(xs[0], ws[0::2], nf, last=False)
        partial = product(xs[1], ws[1::2], nf, partial)
    else:
        partial = product(xs[0], ws, nf)
    parts = lax.all_to_all(
        partial.reshape(nf * nx, count * RB, cols), ("fsdp", "tx"), 0, 0, tiled=True
    ).reshape(nf, nx, count * RB, cols)
    remaining = [held[d][r][e] for d in range(1, nx) for e in range(2) for r in range(1, nx)]
    plan = (tuple(range(nx - 1)),) * (2 * (nx - 1))
    late = base_product(after([owners[2:]], partial)[0], plan, remaining, base_weight, LATE)
    attended, new_keys = merge(parts, near, far, late, *share, new_values.reshape(shape + (cols,)))
    return (attended.reshape(queries.shape), new_keys.reshape(steps, rows, cols))


def solution(mesh):
    nf, nt = mesh.shape["fsdp"], mesh.shape["tp"]
    fine = Mesh(mesh.devices.reshape(nf, nt // 2, 2), ("fsdp", "tx", "core"))
    tp = ("tx", "core")
    in_specs = (
        P(None, "fsdp", tp),
        P(None, "fsdp", tp),
        P("fsdp", None, tp),
        P("fsdp", None, tp),
        P(None, "fsdp", tp),
        P("fsdp"),
        P(None, tp),
        P(("fsdp", "tx", "core"), None),
        P("fsdp", tp),
        P(),
    )
    out_specs = (P(None, "fsdp", tp), P(None, "fsdp", tp))
    return jax.shard_map(
        functools.partial(per_device, nf, nt // 2),
        mesh=fine,
        in_specs=in_specs,
        out_specs=out_specs,
        check_vma=False,
    )
```

```python
import functools
import math

import jax
import jax.numpy as jnp
from jax import lax
from jax.experimental import pallas as pl
from jax.experimental.pallas import tpu as pltpu
from jax.sharding import Mesh
from jax.sharding import PartitionSpec as P

HD = 128
KVH = 8
QH = 128
BLK = 128
GROUP = QH // KVH
RB = 8
MIB = 1024 * 1024
GRANT = 57 * MIB
MIDDLE = 52 * MIB
LATE = 55 * MIB
BESIDE = pl.CostEstimate(flops=0, bytes_accessed=1024, transcendentals=0)
CONTRACT_LAST = (((1,), (1,)), ((), ()))
CONTRACT_FIRST = (((0,), (0,)), ((), ()))


def params(held_bytes):
    return pltpu.CompilerParams(vmem_limit_bytes=min(60 * MIB, 8 * MIB + 2 * held_bytes))


def first_group(part, groups, parts):
    return part * (groups - row_count(groups, parts)) // max(parts - 1, 1)


def row_count(groups, parts):
    return -(-groups // parts)


def scatter_kernel(nx, parts, order_ref, *refs):
    pieces, (out_ref, o_ref, all_ref, sems) = refs[:-4], refs[-4:]
    nf = o_ref.shape[0]
    per_t = all_ref.shape[2] // BLK
    per_f = order_ref.shape[0] // nf
    per_part = o_ref.shape[2] // BLK
    per_own = max(per_part // nx, 1)
    x = lax.axis_index("tx")
    core = lax.axis_index("core")

    def fetch(i):
        piece = pieces[i]
        if len(piece.shape) == 3:
            piece = piece.at[x]
        return pltpu.make_async_copy(piece, all_ref.at[i], sems.at[i])

    def send(f):
        return pltpu.make_async_copy(o_ref.at[f], out_ref.at[f], sems.at[len(pieces) + f])

    for i in range(len(pieces)):
        fetch(i).start()
    for i in range(len(pieces)):
        fetch(i).wait()

    t_bits = per_t.bit_length() - 1
    assert per_t == 1 << t_bits and nx & (nx - 1) == 0
    for f in range(nf):
        for at in range(per_part):
            from_group = f * per_f + at
            if parts > 1:
                chip, rest = at // per_own, at % per_own
                from_group = f * per_f + chip * 2 * per_own + core * per_own + rest
            block = order_ref[from_group]
            owner = lax.shift_right_logical(block, t_bits)
            chip = (lax.shift_right_logical(owner, 1) + nx - x) & (nx - 1)
            index = chip * 2 + ((owner & 1) ^ core)
            lanes = pl.ds(pl.multiple_of((block & (per_t - 1)) * BLK, BLK), BLK)
            o_ref[f, :, at * BLK : (at + 1) * BLK] = all_ref[index, :, lanes]
        send(f).start()
    for f in range(nf):
        send(f).wait()


def scatter(order, pieces, nf, split):
    rows, cols = pieces[-1].shape
    width = len(pieces) * cols // nf // split
    return pl.pallas_call(
        functools.partial(scatter_kernel, len(pieces) // 2, split),
        out_shape=jax.ShapeDtypeStruct((nf, rows, width), jnp.bfloat16),
        in_specs=[pl.BlockSpec(memory_space=pltpu.SMEM)]
        + [pl.BlockSpec(memory_space=pl.ANY)] * len(pieces),
        out_specs=pl.BlockSpec(memory_space=pl.ANY),
        scratch_shapes=[
            pltpu.VMEM((nf, rows, width), jnp.bfloat16),
            pltpu.VMEM((len(pieces), rows, cols), jnp.bfloat16),
            pltpu.SemaphoreType.DMA((len(pieces) + nf,)),
        ],
        compiler_params=params(4 * len(pieces) * rows * cols),
        cost_estimate=pl.CostEstimate(
            flops=0, bytes_accessed=3 * len(pieces) * rows * cols, transcendentals=0
        ),
        name="scatter_columns",
    )(order, *pieces)


def base_kernel(plan, info_ref, base_ref, *refs):
    count = sum(len(targets) for targets in plan)
    made = 1 + max(max(targets) for targets in plan)
    pieces, outs, taken = refs[:count], refs[count : count + made], refs[count + made : -2]
    held, sems = refs[-2:]
    depth = held.shape[1]
    width = taken[0].shape[1]
    chunks = width // depth
    total = held.shape[0]

    def take(i):
        return pltpu.make_async_copy(pieces[i], taken[i], sems.at[total + i])

    def fetch(n):
        row = pl.multiple_of(info_ref[n // chunks] * width + n % chunks * depth, depth)
        return pltpu.make_async_copy(base_ref.at[pl.ds(row, depth), :], held.at[n], sems.at[n])

    firsts = [sum(len(targets) for targets in plan[:q]) for q in range(len(plan))]
    for q, targets in enumerate(plan):
        for r in range(len(targets)):
            take(firsts[q] + r).start()
        for j in range(chunks):
            fetch(q * chunks + j).start()
    sums = [jnp.zeros(o_ref.shape, jnp.float32) for o_ref in outs]
    for q, targets in enumerate(plan):
        for r in range(len(targets)):
            take(firsts[q] + r).wait()
        for j in range(chunks):
            n = q * chunks + j
            fetch(n).wait()
            for r, target in enumerate(targets):
                part = taken[firsts[q] + r][:, j * depth : (j + 1) * depth]
                sums[target] = sums[target] + jnp.dot(
                    part, held[n], preferred_element_type=jnp.float32
                )
    for o_ref, value in zip(outs, sums):
        o_ref[...] = value


def base_product(owners, plan, pieces, base, grant):
    width = pieces[0].shape[1]
    cols = base.shape[1]
    depth = min(width, 1024)
    count = len(plan) * width // depth
    rows = {}
    for target, piece in zip([t for targets in plan for t in targets], pieces):
        rows[target] = piece.shape[0]
    return pl.pallas_call(
        functools.partial(base_kernel, plan),
        out_shape=tuple(
            jax.ShapeDtypeStruct((rows[t], cols), jnp.float32) for t in range(len(rows))
        ),
        in_specs=[pl.BlockSpec(memory_space=pltpu.SMEM)]
        + [pl.BlockSpec(memory_space=pl.ANY)] * (1 + len(pieces)),
        out_specs=(pl.BlockSpec(memory_space=pltpu.VMEM),) * len(rows),
        scratch_shapes=[pltpu.VMEM(piece.shape, jnp.bfloat16) for piece in pieces]
        + [
            pltpu.VMEM((count, depth, cols), jnp.bfloat16),
            pltpu.SemaphoreType.DMA((count + len(pieces),)),
        ],
        compiler_params=pltpu.CompilerParams(vmem_limit_bytes=grant),
        cost_estimate=BESIDE,
        name="base_keys",
    )(owners, base, *pieces)


def scale_kernel(nx, shifts, *refs):
    scales, refs = refs[:nx], refs[nx:]
    pieces, outs = refs[: len(shifts)], refs[len(shifts) :]
    own, cols = pieces[0].shape[1:]
    x = lax.axis_index("tx")
    core = lax.axis_index("core")
    for (d, e), piece, o_ref in zip(shifts, pieces, outs):
        first = (lax.rem(x + d, nx) * 2 + lax.bitwise_xor(core, e)) * (own // BLK)
        for q in range(nx):
            source = lax.rem(q + nx - x, nx)
            for b in range(own // BLK):
                rows = slice(b * BLK, (b + 1) * BLK)
                for c in range(cols // BLK):
                    lanes = slice(c * BLK, (c + 1) * BLK)
                    factor = scales[0][first + b, c]
                    for n in range(1, nx):
                        factor = jnp.where(source == n, scales[n][first + b, c], factor)
                    values = piece[q, rows, lanes].astype(jnp.float32) * factor
                    o_ref[q, rows, lanes] = values.astype(jnp.bfloat16)


def scale_rows(scales, shifts, pieces):
    size = len(pieces) * pieces[0].size
    return pl.pallas_call(
        functools.partial(scale_kernel, pieces[0].shape[0], shifts),
        out_shape=tuple(jax.ShapeDtypeStruct(p.shape, jnp.bfloat16) for p in pieces),
        in_specs=[pl.BlockSpec(memory_space=pltpu.SMEM)] * len(scales)
        + [pl.BlockSpec(memory_space=pltpu.VMEM)] * len(pieces),
        out_specs=(pl.BlockSpec(memory_space=pltpu.VMEM),) * len(pieces),
        compiler_params=params(4 * size),
        cost_estimate=BESIDE,
        name="scale_rows",
    )(*scales, *pieces)


def product_kernel(spread, step, *refs):
    o_ref = refs[-1]
    x_ref, ws = refs[0], refs[1 : 1 + spread]
    earlier = refs[1 + spread : -1]
    nx, own, cols = ws[0].shape
    x = lax.axis_index("tx")
    for q in range(nx):
        total = earlier[0][q] if earlier else jnp.zeros((x_ref.shape[0], cols), jnp.float32)
        for d, w_ref in enumerate(ws):
            at = 0
            if spread > 1:
                at = pl.multiple_of(lax.rem(x + d, nx) * own, BLK)
            total = total + jnp.dot(
                x_ref[:, pl.ds(at, own)], w_ref[q], preferred_element_type=jnp.float32
            )
        if step == "last":
            nf, _, rows, _ = o_ref.shape
            o_ref[:, q] = total.reshape(nf, rows, cols).astype(jnp.bfloat16)
        else:
            o_ref[q] = total


def product(x, ws, nf, earlier=None, last=True):
    total, depth = x.shape
    nx, _, cols = ws[0].shape
    rows = total // nf
    made = nx * total * cols
    read = total * depth + len(ws) * ws[0].size
    before = [] if earlier is None else [earlier]
    out = jax.ShapeDtypeStruct((nx, total, cols), jnp.float32)
    if last:
        out = jax.ShapeDtypeStruct((nf, nx, rows, cols), jnp.bfloat16)
    return pl.pallas_call(
        functools.partial(product_kernel, len(ws), "last" if last else "first"),
        out_shape=out,
        in_specs=[pl.BlockSpec(memory_space=pltpu.VMEM)] * (1 + len(ws) + len(before)),
        out_specs=pl.BlockSpec(memory_space=pltpu.VMEM),
        compiler_params=params(2 * read + 8 * made),
        cost_estimate=pl.CostEstimate(
            flops=2 * made * depth,
            bytes_accessed=2 * read + 6 * made,
            transcendentals=0,
        ),
        name="partial_keys",
    )(x, *ws, *before)


def cached_kernel(len_ref, q_ref, ck_ref, cv_ref, qp_ref, acc_ref, ml_ref):
    step = pl.program_id(0)
    steps, taken = q_ref.shape[:2]
    cap = ck_ref.shape[1]
    heads = ck_ref.shape[2] // HD
    many = steps * GROUP * RB
    factor = 1.0 / math.sqrt(HD)
    place = lax.broadcasted_iota(jnp.int32, (cap, many), 0)
    row = lax.rem(lax.broadcasted_iota(jnp.int32, (cap, many), 1), RB)
    chains = [(i, h) for i in range(taken) for h in range(heads)]
    scores = []
    for i, h in chains:
        lanes = slice(h * HD, (h + 1) * HD)
        q = jnp.concatenate(
            [
                q_ref[s, i, :, (h * GROUP + g) * HD : (h * GROUP + g + 1) * HD].astype(jnp.float32)
                for s in range(steps)
                for g in range(GROUP)
            ],
            axis=0,
        ).astype(jnp.bfloat16)
        qp_ref[i, h] = q
        k = ck_ref[i * RB : (i + 1) * RB, :, lanes].reshape(RB * cap, HD)
        scores.append(
            lax.dot_general(k, q, CONTRACT_LAST, preferred_element_type=jnp.float32)
        )
    weights = []
    for (i, h), sc in zip(chains, scores):
        if h == 0:
            bias = jnp.concatenate(
                [
                    jnp.where(
                        (row == r) & (place < len_ref[(step * taken + i) * RB + r]), 0.0, -1e30
                    )
                    for r in range(RB)
                ],
                axis=0,
            )
        sc = sc * factor + bias
        top = jnp.max(sc, axis=0, keepdims=True)
        expo = jnp.exp(sc - top)
        ml_ref[i, h, 0:1, :] = top
        ml_ref[i, h, 1:2, :] = jnp.sum(expo, axis=0, keepdims=True)
        weights.append(expo.astype(jnp.bfloat16))
    for (i, h), expo in zip(chains, weights):
        v = cv_ref[i * RB : (i + 1) * RB, :, h * HD : (h + 1) * HD].reshape(RB * cap, HD)
        acc_ref[i, h] = lax.dot_general(
            v, expo, CONTRACT_FIRST, preferred_element_type=jnp.float32
        ).astype(jnp.bfloat16)


def taken_at_once(batches):
    return 3 if batches % 3 == 0 else 1


def cached(lengths, queries, cache_keys, cache_values):
    steps, batches, _, width = queries.shape
    cap, cols = cache_keys.shape[1:]
    heads = cols // HD
    many = steps * GROUP * RB
    n = taken_at_once(batches)
    return pl.pallas_call(
        cached_kernel,
        grid=(batches // n,),
        out_shape=(
            jax.ShapeDtypeStruct((batches, heads, many, HD), jnp.bfloat16),
            jax.ShapeDtypeStruct((batches, heads, HD, many), jnp.bfloat16),
            jax.ShapeDtypeStruct((batches, heads, 2, many), jnp.float32),
        ),
        in_specs=[
            pl.BlockSpec(memory_space=pltpu.SMEM),
            pl.BlockSpec((steps, n, RB, width), lambda i: (0, i, 0, 0)),
            pl.BlockSpec((n * RB, cap, cols), lambda i: (i, 0, 0)),
            pl.BlockSpec((n * RB, cap, cols), lambda i: (i, 0, 0)),
        ],
        out_specs=(
            pl.BlockSpec((n, heads, many, HD), lambda i: (i, 0, 0, 0)),
            pl.BlockSpec((n, heads, HD, many), lambda i: (i, 0, 0, 0)),
            pl.BlockSpec((n, heads, 2, many), lambda i: (i, 0, 0, 0)),
        ),
        compiler_params=pltpu.CompilerParams(vmem_limit_bytes=MIDDLE),
        cost_estimate=BESIDE,
        name="attend_cached",
    )(lengths, queries, cache_keys, cache_values)


def merge_kernel(nx, taken, *refs):
    count = nx + 6
    sources, (out_ref, nk_ref), held_refs = refs[:count], refs[count : count + 2], refs[count + 2 :]
    here, (o_ref, held, eye, sems) = held_refs[:count], held_refs[count:]
    parts_ref, near_ref, far_ref = here[:3]
    late_refs, (nv_ref, qp_ref, acc_ref, ml_ref) = here[3 : nx + 2], here[nx + 2 :]
    steps, batches = nk_ref.shape[0], nk_ref.shape[1]
    heads = acc_ref.shape[1]
    many = steps * GROUP * RB
    factor = 1.0 / math.sqrt(HD)
    groups = batches // taken

    copies = [
        pltpu.make_async_copy(sources[i], here[i], sems.at[i]) for i in range(count - 3)
    ]
    shares = []
    for step in range(groups):
        rows = pl.ds(step * taken, taken)
        shares.append(
            [
                pltpu.make_async_copy(
                    sources[i].at[rows], here[i].at[rows], sems.at[i + 3 * step]
                )
                for i in range(count - 3, count)
            ]
        )
    for copy in [*copies, *(copy for share in shares for copy in share)]:
        copy.start()

    line = lax.broadcasted_iota(jnp.int32, (many, many), 0)
    lane = lax.broadcasted_iota(jnp.int32, (many, many), 1)
    eye[...] = jnp.where(line == lane, 1.0, 0.0).astype(jnp.bfloat16)
    for copy in copies:
        copy.wait()
    me = lax.axis_index("tx")
    for x in range(nx):
        for k in range(parts_ref.shape[2] // RB):
            g = first_group(x, steps * batches, nx) + k
            rows = slice(k * RB, (k + 1) * RB)
            at = lax.rem(x + nx - me, nx)
            total = near_ref[g * RB : (g + 1) * RB, :]
            far = far_ref[rows, :]
            for r, late_ref in enumerate(late_refs):
                far = jnp.where(at == r + 1, late_ref[rows, :], far)
            total = total + far
            for f in range(parts_ref.shape[0]):
                total = total + parts_ref[f, x, rows, :].astype(jnp.float32)
            rounded = total.astype(jnp.bfloat16)
            nk_ref[g // batches, g % batches] = rounded
            held[g // batches, g % batches] = rounded.astype(jnp.float32)

    key = lax.broadcasted_iota(jnp.int32, (steps * RB, many), 0)
    lane = lax.broadcasted_iota(jnp.int32, (steps * RB, many), 1)
    same_row = lax.rem(key, RB) == lax.rem(lane, RB)
    known = lax.div(key, RB) <= lax.div(lane, GROUP * RB)
    bias = jnp.where(same_row & known, 0.0, -1e30)
    leaving = []
    for step in range(groups):
        first = step * taken
        for copy in shares[step]:
            copy.wait()
        chains = [(i, h) for i in range(first, first + taken) for h in range(heads)]
        scores = []
        for i, h in chains:
            lanes = slice(h * HD, (h + 1) * HD)
            keys = jnp.concatenate([held[u, i, :, lanes] for u in range(steps)], axis=0)
            scores.append(
                lax.dot_general(
                    keys.astype(jnp.bfloat16),
                    qp_ref[i, h],
                    CONTRACT_LAST,
                    preferred_element_type=jnp.float32,
                )
            )
        added, scales = [], []
        for (i, h), sn in zip(chains, scores):
            lanes = slice(h * HD, (h + 1) * HD)
            values = jnp.concatenate(
                [nv_ref[u, i, :, lanes].astype(jnp.float32) for u in range(steps)], axis=0
            )
            sn = sn * factor + bias
            old = ml_ref[i, h, 0:1, :]
            top = jnp.maximum(old, jnp.max(sn, axis=0, keepdims=True))
            keep = jnp.exp(old - top)
            expo = jnp.exp(sn - top)
            whole = ml_ref[i, h, 1:2, :] * keep + jnp.sum(expo, axis=0, keepdims=True)
            inverse = 1.0 / whole
            scales.append(keep * inverse)
            added.append(
                lax.dot_general(
                    values.astype(jnp.bfloat16),
                    (expo * inverse).astype(jnp.bfloat16),
                    CONTRACT_FIRST,
                    preferred_element_type=jnp.float32,
                )
            )
        turned = [
            (acc_ref[i, h].astype(jnp.float32) * scale + more).astype(jnp.bfloat16)
            for (i, h), scale, more in zip(chains, scales, added)
        ]
        for (i, h), out in zip(chains, turned):
            out = lax.dot_general(
                eye[...], out, CONTRACT_LAST, preferred_element_type=jnp.float32
            ).astype(jnp.bfloat16)
            for s in range(steps):
                for g in range(GROUP):
                    at = (s * GROUP + g) * RB
                    o_ref[s, i, :, (h * GROUP + g) * HD : (h * GROUP + g + 1) * HD] = out[
                        at : at + RB
                    ]
        rows = pl.ds(first, taken)
        leaving.append(
            pltpu.make_async_copy(
                o_ref.at[:, rows], out_ref.at[:, rows], sems.at[count + 3 * groups + step]
            )
        )
        leaving[-1].start()
    for copy in leaving:
        copy.wait()


def merge(parts, near, far, late, packed, sums, tops, new_values):
    batches, heads, many, _ = packed.shape
    steps = new_values.shape[0]
    width = many // steps // RB * heads * HD
    n = taken_at_once(batches)
    made = jax.ShapeDtypeStruct((steps, batches, RB, width), jnp.bfloat16)
    operands = [parts, near, far, *late, new_values, packed, sums, tops]
    return pl.pallas_call(
        functools.partial(merge_kernel, parts.shape[1], n),
        out_shape=(made, jax.ShapeDtypeStruct(new_values.shape, jnp.bfloat16)),
        in_specs=[pl.BlockSpec(memory_space=pl.ANY)] * len(operands),
        out_specs=(
            pl.BlockSpec(memory_space=pl.ANY),
            pl.BlockSpec(memory_space=pltpu.VMEM),
        ),
        scratch_shapes=[pltpu.VMEM(operand.shape, operand.dtype) for operand in operands]
        + [
            pltpu.VMEM(made.shape, made.dtype),
            pltpu.VMEM(new_values.shape, jnp.float32),
            pltpu.VMEM((many, many), jnp.bfloat16),
            pltpu.SemaphoreType.DMA((len(operands) + 4 * (batches // n),)),
        ],
        compiler_params=pltpu.CompilerParams(vmem_limit_bytes=GRANT),
        cost_estimate=pl.CostEstimate(
            flops=4 * packed.size * many,
            bytes_accessed=8 * packed.size + 4 * parts.size,
            transcendentals=packed.size // 8,
        ),
        name="attend_new",
    )(*operands)


def shift_of(nx, d):
    return [(s, (s - d) % nx) for s in range(nx)]


def part_of(array, start, size, dim):
    starts = [0] * array.ndim
    starts[dim] = start
    sizes = list(array.shape)
    sizes[dim] = size
    return lax.dynamic_slice(array, starts, sizes, allow_negative_indices=False)


def after(arrays, earlier):
    return list(lax.optimization_barrier((*arrays, earlier))[:-1])


def swap(piece):
    return lax.ppermute(piece, "core", [(0, 1), (1, 0)])


def per_device(
    nf,
    nx,
    hidden,
    queries,
    cache_keys,
    cache_values,
    new_values,
    lengths,
    base_weight,
    delta_values,
    delta_scales,
    block_order,
):
    steps, rows, width = hidden.shape
    cols = base_weight.shape[1]
    batches = rows // RB
    count = row_count(steps * batches, nx)
    x = lax.axis_index("tx")
    core = lax.axis_index("core")
    depth = 2 * nx * width // nf
    own = delta_values.shape[0]
    split = 2 if own % BLK == 0 else 1

    def to_shift(d, e):
        return [(s * 2 + c, (s - d) % nx * 2 + (c ^ e)) for s in range(nx) for c in range(2)]

    shifts = [(d, e) for d in range(nx) for e in range(2)]
    sent = []
    for e in range(2):
        to = lax.bitwise_xor(core, e)
        sent.append(
            jnp.stack([part_of(delta_values, (2 * q + to) * cols, cols, 1) for q in range(nx)])
        )
    scales = [delta_scales.astype(jnp.float32)]
    scales += [lax.ppermute(scales[0], "tx", shift_of(nx, d)) for d in range(1, nx)]

    flat = hidden.reshape(steps * rows, width)
    whole_rows = swap(flat)

    def rows_of(array, d):
        start = first_group(lax.rem(x + d, nx), steps * batches, nx) * RB
        return part_of(array, start, count * RB, 0)

    held = [[None] * nx for _ in range(nx)]
    for d in range(1, nx):
        came = lax.ppermute(rows_of(flat, (-d) % nx), "tx", shift_of(nx, d))
        ready = [came]
        for early in (*sent, scales[d]):
            ready = after(ready, early)
        held[d][0] = (came, swap(ready[0]))
    if nx == steps and count * RB == rows:
        pieces = [hidden, whole_rows.reshape(hidden.shape)]
    else:
        pieces = [rows_of(flat, 0), rows_of(whole_rows, 0)]
    pieces += [p for d in range(1, nx) for p in held[d][0]]
    mine = scatter(block_order, pieces, nf, split)

    behind = after(sent, held[-1][0][0])
    ws = [sent[0]]
    for d, e in shifts[1:]:
        ws.append(lax.ppermute((behind if d else sent)[e], ("tx", "core"), to_shift(d, e)))
    arrived = ws[1:]
    if split > 1:
        ws[:2] = scale_rows(scales, shifts[:2], ws[:2])
    if split == 1:
        by_chip = jnp.repeat(jnp.roll(jnp.stack(scales), x, axis=0), BLK, axis=2)
        whole = jnp.zeros((nx, depth, cols), jnp.bfloat16)
        for (d, e), piece in zip(shifts, ws):
            at = (lax.rem(x + d, nx) * 2 + lax.bitwise_xor(core, e)) * own
            factor = jnp.take(by_chip, (at + jnp.arange(own)) // BLK, axis=1)
            piece = (piece.astype(jnp.float32) * factor).astype(jnp.bfloat16)
            whole = lax.dynamic_update_slice_in_dim(whole, piece, at, 1)
        ws = [whole]

    (soon,) = after([flat], mine)
    late = []
    for d in range(1, nx):
        for r in range(1, nx):
            start = first_group(lax.rem(x + (r - d) % nx, nx), steps * batches, nx) * RB
            late.append(part_of(soon, start, count * RB, 0))
            (piece,) = after(late[-1:], arrived[-1])
            came = lax.ppermute(piece, "tx", shift_of(nx, d))
            held[d][r] = (came, swap(came))

    owners = [lax.rem(x + d, nx) * 2 + lax.bitwise_xor(core, e) for d, e in shifts]
    owners = jnp.stack(owners)
    first, then = after([owners, lengths], mine)
    for piece in (*late, *ws[:1]):
        (first,) = after([first], piece)
    early = [held[d][0][e] for d in range(1, nx) for e in range(2)]
    plan = ((0,),) * 2 + ((1,),) * len(early)
    near, far = base_product(first, plan, [flat, whole_rows, *early], base_weight, MIDDLE)
    shape = (steps, batches, RB)
    share = cached(
        then, queries.reshape(shape + queries.shape[2:]), cache_keys, cache_values
    )
    if split > 1:
        for earlier in (near, far, share[0]):
            scales = after(scales, earlier)
        ws[2:] = scale_rows(scales, shifts[2:], ws[2:])
    mine = lax.all_to_all(mine, "fsdp", 0, 0, tiled=True)
    xs = [mine.reshape(nf * count * RB, depth // split)]
    for earlier in (*arrived[:1], *ws[-2:], near, far, share[0]):
        xs = after(xs, earlier)
    if split > 1:
        xs.append(swap(xs[0]))
        partial = product(xs[0], ws[0::2], nf, last=False)
        partial = product(xs[1], ws[1::2], nf, partial)
    else:
        partial = product(xs[0], ws, nf)
    parts = lax.all_to_all(
        partial.reshape(nf * nx, count * RB, cols), ("fsdp", "tx"), 0, 0, tiled=True
    ).reshape(nf, nx, count * RB, cols)
    remaining = [held[d][r][e] for d in range(1, nx) for e in range(2) for r in range(1, nx)]
    plan = (tuple(range(nx - 1)),) * (2 * (nx - 1))
    late = base_product(after([owners[2:]], partial)[0], plan, remaining, base_weight, LATE)
    attended, new_keys = merge(parts, near, far, late, *share, new_values.reshape(shape + (cols,)))
    return (attended.reshape(queries.shape), new_keys.reshape(steps, rows, cols))


def solution(mesh):
    nf, nt = mesh.shape["fsdp"], mesh.shape["tp"]
    fine = Mesh(mesh.devices.reshape(nf, nt // 2, 2), ("fsdp", "tx", "core"))
    tp = ("tx", "core")
    in_specs = (
        P(None, "fsdp", tp),
        P(None, "fsdp", tp),
        P("fsdp", None, tp),
        P("fsdp", None, tp),
        P(None, "fsdp", tp),
        P("fsdp"),
        P(None, tp),
        P(("fsdp", "tx", "core"), None),
        P("fsdp", tp),
        P(),
    )
    out_specs = (P(None, "fsdp", tp), P(None, "fsdp", tp))
    return jax.shard_map(
        functools.partial(per_device, nf, nt // 2),
        mesh=fine,
        in_specs=in_specs,
        out_specs=out_specs,
        check_vma=False,
    )
```

```python
import functools
import math

import jax
import jax.numpy as jnp
from jax import lax
from jax.experimental import pallas as pl
from jax.experimental.pallas import tpu as pltpu
from jax.sharding import Mesh
from jax.sharding import PartitionSpec as P

HD = 128
KVH = 8
QH = 128
BLK = 128
GROUP = QH // KVH
RB = 8
MIB = 1024 * 1024
GRANT = 57 * MIB
MIDDLE = 52 * MIB
LATE = 55 * MIB
BESIDE = pl.CostEstimate(flops=0, bytes_accessed=1024, transcendentals=0)
CONTRACT_LAST = (((1,), (1,)), ((), ()))
CONTRACT_FIRST = (((0,), (0,)), ((), ()))


def params(held_bytes):
    return pltpu.CompilerParams(vmem_limit_bytes=min(60 * MIB, 8 * MIB + 2 * held_bytes))


def first_group(part, groups, parts):
    return part * (groups - row_count(groups, parts)) // max(parts - 1, 1)


def row_count(groups, parts):
    return -(-groups // parts)


def scatter_kernel(nx, parts, order_ref, *refs):
    pieces, (out_ref, o_ref, all_ref, sems) = refs[:-4], refs[-4:]
    nf = o_ref.shape[0]
    per_t = all_ref.shape[2] // BLK
    per_f = order_ref.shape[0] // nf
    per_part = o_ref.shape[2] // BLK
    per_own = max(per_part // nx, 1)
    x = lax.axis_index("tx")
    core = lax.axis_index("core")

    def fetch(i):
        piece = pieces[i]
        if len(piece.shape) == 3:
            piece = piece.at[x]
        return pltpu.make_async_copy(piece, all_ref.at[i], sems.at[i])

    def send(f):
        return pltpu.make_async_copy(o_ref.at[f], out_ref.at[f], sems.at[len(pieces) + f])

    for i in range(len(pieces)):
        fetch(i).start()
    for i in range(len(pieces)):
        fetch(i).wait()

    t_bits = per_t.bit_length() - 1
    assert per_t == 1 << t_bits and nx & (nx - 1) == 0
    for f in range(nf):
        for at in range(per_part):
            from_group = f * per_f + at
            if parts > 1:
                chip, rest = at // per_own, at % per_own
                from_group = f * per_f + chip * 2 * per_own + core * per_own + rest
            block = order_ref[from_group]
            owner = lax.shift_right_logical(block, t_bits)
            chip = (lax.shift_right_logical(owner, 1) + nx - x) & (nx - 1)
            index = chip * 2 + ((owner & 1) ^ core)
            lanes = pl.ds(pl.multiple_of((block & (per_t - 1)) * BLK, BLK), BLK)
            o_ref[f, :, at * BLK : (at + 1) * BLK] = all_ref[index, :, lanes]
        send(f).start()
    for f in range(nf):
        send(f).wait()


def scatter(order, pieces, nf, split):
    rows, cols = pieces[-1].shape
    width = len(pieces) * cols // nf // split
    return pl.pallas_call(
        functools.partial(scatter_kernel, len(pieces) // 2, split),
        out_shape=jax.ShapeDtypeStruct((nf, rows, width), jnp.bfloat16),
        in_specs=[pl.BlockSpec(memory_space=pltpu.SMEM)]
        + [pl.BlockSpec(memory_space=pl.ANY)] * len(pieces),
        out_specs=pl.BlockSpec(memory_space=pl.ANY),
        scratch_shapes=[
            pltpu.VMEM((nf, rows, width), jnp.bfloat16),
            pltpu.VMEM((len(pieces), rows, cols), jnp.bfloat16),
            pltpu.SemaphoreType.DMA((len(pieces) + nf,)),
        ],
        compiler_params=params(4 * len(pieces) * rows * cols),
        cost_estimate=pl.CostEstimate(
            flops=0, bytes_accessed=3 * len(pieces) * rows * cols, transcendentals=0
        ),
        name="scatter_columns",
    )(order, *pieces)


def base_kernel(plan, info_ref, base_ref, *refs):
    count = sum(len(targets) for targets in plan)
    made = 1 + max(max(targets) for targets in plan)
    pieces, outs, taken = refs[:count], refs[count : count + made], refs[count + made : -2]
    held, sems = refs[-2:]
    depth = held.shape[1]
    width = taken[0].shape[1]
    chunks = width // depth
    total = held.shape[0]

    def take(i):
        return pltpu.make_async_copy(pieces[i], taken[i], sems.at[total + i])

    def fetch(n):
        row = pl.multiple_of(info_ref[n // chunks] * width + n % chunks * depth, depth)
        return pltpu.make_async_copy(base_ref.at[pl.ds(row, depth), :], held.at[n], sems.at[n])

    firsts = [sum(len(targets) for targets in plan[:q]) for q in range(len(plan))]
    for q, targets in enumerate(plan):
        for r in range(len(targets)):
            take(firsts[q] + r).start()
        for j in range(chunks):
            fetch(q * chunks + j).start()
    sums = [jnp.zeros(o_ref.shape, jnp.float32) for o_ref in outs]
    for q, targets in enumerate(plan):
        for r in range(len(targets)):
            take(firsts[q] + r).wait()
        for j in range(chunks):
            n = q * chunks + j
            fetch(n).wait()
            for r, target in enumerate(targets):
                part = taken[firsts[q] + r][:, j * depth : (j + 1) * depth]
                sums[target] = sums[target] + jnp.dot(
                    part, held[n], preferred_element_type=jnp.float32
                )
    for o_ref, value in zip(outs, sums):
        o_ref[...] = value


def base_product(owners, plan, pieces, base, grant):
    width = pieces[0].shape[1]
    cols = base.shape[1]
    depth = min(width, 1024)
    count = len(plan) * width // depth
    rows = {}
    for target, piece in zip([t for targets in plan for t in targets], pieces):
        rows[target] = piece.shape[0]
    return pl.pallas_call(
        functools.partial(base_kernel, plan),
        out_shape=tuple(
            jax.ShapeDtypeStruct((rows[t], cols), jnp.float32) for t in range(len(rows))
        ),
        in_specs=[pl.BlockSpec(memory_space=pltpu.SMEM)]
        + [pl.BlockSpec(memory_space=pl.ANY)] * (1 + len(pieces)),
        out_specs=(pl.BlockSpec(memory_space=pltpu.VMEM),) * len(rows),
        scratch_shapes=[pltpu.VMEM(piece.shape, jnp.bfloat16) for piece in pieces]
        + [
            pltpu.VMEM((count, depth, cols), jnp.bfloat16),
            pltpu.SemaphoreType.DMA((count + len(pieces),)),
        ],
        compiler_params=pltpu.CompilerParams(vmem_limit_bytes=grant),
        cost_estimate=BESIDE,
        name="base_keys",
    )(owners, base, *pieces)


def scale_kernel(nx, shifts, *refs):
    scales, refs = refs[:nx], refs[nx:]
    pieces, outs = refs[: len(shifts)], refs[len(shifts) :]
    own, cols = pieces[0].shape[1:]
    x = lax.axis_index("tx")
    core = lax.axis_index("core")
    for (d, e), piece, o_ref in zip(shifts, pieces, outs):
        first = (lax.rem(x + d, nx) * 2 + lax.bitwise_xor(core, e)) * (own // BLK)
        for q in range(nx):
            source = lax.rem(q + nx - x, nx)
            for b in range(own // BLK):
                rows = slice(b * BLK, (b + 1) * BLK)
                for c in range(cols // BLK):
                    lanes = slice(c * BLK, (c + 1) * BLK)
                    factor = scales[0][first + b, c]
                    for n in range(1, nx):
                        factor = jnp.where(source == n, scales[n][first + b, c], factor)
                    values = piece[q, rows, lanes].astype(jnp.float32) * factor
                    o_ref[q, rows, lanes] = values.astype(jnp.bfloat16)


def scale_rows(scales, shifts, pieces):
    size = len(pieces) * pieces[0].size
    return pl.pallas_call(
        functools.partial(scale_kernel, pieces[0].shape[0], shifts),
        out_shape=tuple(jax.ShapeDtypeStruct(p.shape, jnp.bfloat16) for p in pieces),
        in_specs=[pl.BlockSpec(memory_space=pltpu.SMEM)] * len(scales)
        + [pl.BlockSpec(memory_space=pltpu.VMEM)] * len(pieces),
        out_specs=(pl.BlockSpec(memory_space=pltpu.VMEM),) * len(pieces),
        compiler_params=params(4 * size),
        cost_estimate=BESIDE,
        name="scale_rows",
    )(*scales, *pieces)


def product_kernel(spread, step, *refs):
    o_ref = refs[-1]
    x_ref, ws = refs[0], refs[1 : 1 + spread]
    earlier = refs[1 + spread : -1]
    nx, own, cols = ws[0].shape
    x = lax.axis_index("tx")
    for q in range(nx):
        total = earlier[0][q] if earlier else jnp.zeros((x_ref.shape[0], cols), jnp.float32)
        for d, w_ref in enumerate(ws):
            at = 0
            if spread > 1:
                at = pl.multiple_of(lax.rem(x + d, nx) * own, BLK)
            total = total + jnp.dot(
                x_ref[:, pl.ds(at, own)], w_ref[q], preferred_element_type=jnp.float32
            )
        if step == "last":
            nf, _, rows, _ = o_ref.shape
            o_ref[:, q] = total.reshape(nf, rows, cols).astype(jnp.bfloat16)
        else:
            o_ref[q] = total


def product(x, ws, nf, earlier=None, last=True):
    total, depth = x.shape
    nx, _, cols = ws[0].shape
    rows = total // nf
    made = nx * total * cols
    read = total * depth + len(ws) * ws[0].size
    before = [] if earlier is None else [earlier]
    out = jax.ShapeDtypeStruct((nx, total, cols), jnp.float32)
    if last:
        out = jax.ShapeDtypeStruct((nf, nx, rows, cols), jnp.bfloat16)
    return pl.pallas_call(
        functools.partial(product_kernel, len(ws), "last" if last else "first"),
        out_shape=out,
        in_specs=[pl.BlockSpec(memory_space=pltpu.VMEM)] * (1 + len(ws) + len(before)),
        out_specs=pl.BlockSpec(memory_space=pltpu.VMEM),
        compiler_params=params(2 * read + 8 * made),
        cost_estimate=pl.CostEstimate(
            flops=2 * made * depth,
            bytes_accessed=2 * read + 6 * made,
            transcendentals=0,
        ),
        name="partial_keys",
    )(x, *ws, *before)


def cached_kernel(len_ref, q_ref, ck_ref, cv_ref, qp_ref, acc_ref, ml_ref):
    step = pl.program_id(0)
    steps, taken = q_ref.shape[:2]
    cap = ck_ref.shape[1]
    heads = ck_ref.shape[2] // HD
    many = steps * GROUP * RB
    factor = 1.0 / math.sqrt(HD)
    place = lax.broadcasted_iota(jnp.int32, (cap, many), 0)
    row = lax.rem(lax.broadcasted_iota(jnp.int32, (cap, many), 1), RB)
    chains = [(i, h) for i in range(taken) for h in range(heads)]
    scores = []
    for i, h in chains:
        lanes = slice(h * HD, (h + 1) * HD)
        q = jnp.concatenate(
            [
                q_ref[s, i, :, (h * GROUP + g) * HD : (h * GROUP + g + 1) * HD].astype(jnp.float32)
                for s in range(steps)
                for g in range(GROUP)
            ],
            axis=0,
        ).astype(jnp.bfloat16)
        qp_ref[i, h] = q
        k = ck_ref[i * RB : (i + 1) * RB, :, lanes].reshape(RB * cap, HD)
        scores.append(
            lax.dot_general(k, q, CONTRACT_LAST, preferred_element_type=jnp.float32)
        )
    weights = []
    for (i, h), sc in zip(chains, scores):
        if h == 0:
            bias = jnp.concatenate(
                [
                    jnp.where(
                        (row == r) & (place < len_ref[(step * taken + i) * RB + r]), 0.0, -1e30
                    )
                    for r in range(RB)
                ],
                axis=0,
            )
        sc = sc * factor + bias
        top = jnp.max(sc, axis=0, keepdims=True)
        expo = jnp.exp(sc - top)
        ml_ref[i, h, 0:1, :] = top
        ml_ref[i, h, 1:2, :] = jnp.sum(expo, axis=0, keepdims=True)
        weights.append(expo.astype(jnp.bfloat16))
    for (i, h), expo in zip(chains, weights):
        v = cv_ref[i * RB : (i + 1) * RB, :, h * HD : (h + 1) * HD].reshape(RB * cap, HD)
        acc_ref[i, h] = lax.dot_general(
            v, expo, CONTRACT_FIRST, preferred_element_type=jnp.float32
        )


def taken_at_once(batches):
    return 3 if batches % 3 == 0 else 1


def cached(lengths, queries, cache_keys, cache_values):
    steps, batches, _, width = queries.shape
    cap, cols = cache_keys.shape[1:]
    heads = cols // HD
    many = steps * GROUP * RB
    n = taken_at_once(batches)
    return pl.pallas_call(
        cached_kernel,
        grid=(batches // n,),
        out_shape=(
            jax.ShapeDtypeStruct((batches, heads, many, HD), jnp.bfloat16),
            jax.ShapeDtypeStruct((batches, heads, HD, many), jnp.float32),
            jax.ShapeDtypeStruct((batches, heads, 2, many), jnp.float32),
        ),
        in_specs=[
            pl.BlockSpec(memory_space=pltpu.SMEM),
            pl.BlockSpec((steps, n, RB, width), lambda i: (0, i, 0, 0)),
            pl.BlockSpec((n * RB, cap, cols), lambda i: (i, 0, 0)),
            pl.BlockSpec((n * RB, cap, cols), lambda i: (i, 0, 0)),
        ],
        out_specs=(
            pl.BlockSpec((n, heads, many, HD), lambda i: (i, 0, 0, 0)),
            pl.BlockSpec((n, heads, HD, many), lambda i: (i, 0, 0, 0)),
            pl.BlockSpec((n, heads, 2, many), lambda i: (i, 0, 0, 0)),
        ),
        compiler_params=pltpu.CompilerParams(vmem_limit_bytes=MIDDLE),
        cost_estimate=BESIDE,
        name="attend_cached",
    )(lengths, queries, cache_keys, cache_values)


def merge_kernel(nx, taken, *refs):
    count = nx + 6
    sources, (out_ref, nk_ref), held_refs = refs[:count], refs[count : count + 2], refs[count + 2 :]
    here, (o_ref, held, eye, sems) = held_refs[:count], held_refs[count:]
    parts_ref, near_ref, far_ref = here[:3]
    late_refs, (nv_ref, qp_ref, acc_ref, ml_ref) = here[3 : nx + 2], here[nx + 2 :]
    steps, batches = nk_ref.shape[0], nk_ref.shape[1]
    heads = acc_ref.shape[1]
    many = steps * GROUP * RB
    factor = 1.0 / math.sqrt(HD)
    groups = batches // taken

    copies = [
        pltpu.make_async_copy(sources[i], here[i], sems.at[i]) for i in range(count - 3)
    ]
    shares = []
    for step in range(groups):
        rows = pl.ds(step * taken, taken)
        shares.append(
            [
                pltpu.make_async_copy(
                    sources[i].at[rows], here[i].at[rows], sems.at[i + 3 * step]
                )
                for i in range(count - 3, count)
            ]
        )
    for copy in [*copies, *(copy for share in shares for copy in share)]:
        copy.start()

    line = lax.broadcasted_iota(jnp.int32, (many, many), 0)
    lane = lax.broadcasted_iota(jnp.int32, (many, many), 1)
    eye[...] = jnp.where(line == lane, 1.0, 0.0).astype(jnp.bfloat16)
    for copy in copies:
        copy.wait()
    me = lax.axis_index("tx")
    for x in range(nx):
        for k in range(parts_ref.shape[2] // RB):
            g = first_group(x, steps * batches, nx) + k
            rows = slice(k * RB, (k + 1) * RB)
            at = lax.rem(x + nx - me, nx)
            total = near_ref[g * RB : (g + 1) * RB, :]
            far = far_ref[rows, :]
            for r, late_ref in enumerate(late_refs):
                far = jnp.where(at == r + 1, late_ref[rows, :], far)
            total = total + far
            for f in range(parts_ref.shape[0]):
                total = total + parts_ref[f, x, rows, :].astype(jnp.float32)
            rounded = total.astype(jnp.bfloat16)
            nk_ref[g // batches, g % batches] = rounded
            held[g // batches, g % batches] = rounded.astype(jnp.float32)

    key = lax.broadcasted_iota(jnp.int32, (steps * RB, many), 0)
    lane = lax.broadcasted_iota(jnp.int32, (steps * RB, many), 1)
    same_row = lax.rem(key, RB) == lax.rem(lane, RB)
    known = lax.div(key, RB) <= lax.div(lane, GROUP * RB)
    bias = jnp.where(same_row & known, 0.0, -1e30)
    leaving = []
    for step in range(groups):
        first = step * taken
        for copy in shares[step]:
            copy.wait()
        chains = [(i, h) for i in range(first, first + taken) for h in range(heads)]
        scores = []
        for i, h in chains:
            lanes = slice(h * HD, (h + 1) * HD)
            keys = jnp.concatenate([held[u, i, :, lanes] for u in range(steps)], axis=0)
            scores.append(
                lax.dot_general(
                    keys.astype(jnp.bfloat16),
                    qp_ref[i, h],
                    CONTRACT_LAST,
                    preferred_element_type=jnp.float32,
                )
            )
        added, scales = [], []
        for (i, h), sn in zip(chains, scores):
            lanes = slice(h * HD, (h + 1) * HD)
            values = jnp.concatenate(
                [nv_ref[u, i, :, lanes].astype(jnp.float32) for u in range(steps)], axis=0
            )
            sn = sn * factor + bias
            old = ml_ref[i, h, 0:1, :]
            top = jnp.maximum(old, jnp.max(sn, axis=0, keepdims=True))
            keep = jnp.exp(old - top)
            expo = jnp.exp(sn - top)
            whole = ml_ref[i, h, 1:2, :] * keep + jnp.sum(expo, axis=0, keepdims=True)
            inverse = 1.0 / whole
            scales.append(keep * inverse)
            added.append(
                lax.dot_general(
                    values.astype(jnp.bfloat16),
                    (expo * inverse).astype(jnp.bfloat16),
                    CONTRACT_FIRST,
                    preferred_element_type=jnp.float32,
                )
            )
        turned = [
            (acc_ref[i, h] * scale + more).astype(jnp.bfloat16)
            for (i, h), scale, more in zip(chains, scales, added)
        ]
        for (i, h), out in zip(chains, turned):
            out = lax.dot_general(
                eye[...], out, CONTRACT_LAST, preferred_element_type=jnp.float32
            ).astype(jnp.bfloat16)
            for s in range(steps):
                for g in range(GROUP):
                    at = (s * GROUP + g) * RB
                    o_ref[s, i, :, (h * GROUP + g) * HD : (h * GROUP + g + 1) * HD] = out[
                        at : at + RB
                    ]
        rows = pl.ds(first, taken)
        leaving.append(
            pltpu.make_async_copy(
                o_ref.at[:, rows], out_ref.at[:, rows], sems.at[count + 3 * groups + step]
            )
        )
        leaving[-1].start()
    for copy in leaving:
        copy.wait()


def merge(parts, near, far, late, packed, sums, tops, new_values):
    batches, heads, many, _ = packed.shape
    steps = new_values.shape[0]
    width = many // steps // RB * heads * HD
    n = taken_at_once(batches)
    made = jax.ShapeDtypeStruct((steps, batches, RB, width), jnp.bfloat16)
    operands = [parts, near, far, *late, new_values, packed, sums, tops]
    return pl.pallas_call(
        functools.partial(merge_kernel, parts.shape[1], n),
        out_shape=(made, jax.ShapeDtypeStruct(new_values.shape, jnp.bfloat16)),
        in_specs=[pl.BlockSpec(memory_space=pl.ANY)] * len(operands),
        out_specs=(
            pl.BlockSpec(memory_space=pl.ANY),
            pl.BlockSpec(memory_space=pltpu.VMEM),
        ),
        scratch_shapes=[pltpu.VMEM(operand.shape, operand.dtype) for operand in operands]
        + [
            pltpu.VMEM(made.shape, made.dtype),
            pltpu.VMEM(new_values.shape, jnp.float32),
            pltpu.VMEM((many, many), jnp.bfloat16),
            pltpu.SemaphoreType.DMA((len(operands) + 4 * (batches // n),)),
        ],
        compiler_params=pltpu.CompilerParams(vmem_limit_bytes=GRANT),
        cost_estimate=pl.CostEstimate(
            flops=4 * packed.size * many,
            bytes_accessed=8 * packed.size + 4 * parts.size,
            transcendentals=packed.size // 8,
        ),
        name="attend_new",
    )(*operands)


def shift_of(nx, d):
    return [(s, (s - d) % nx) for s in range(nx)]


def part_of(array, start, size, dim):
    starts = [0] * array.ndim
    starts[dim] = start
    sizes = list(array.shape)
    sizes[dim] = size
    return lax.dynamic_slice(array, starts, sizes, allow_negative_indices=False)


def after(arrays, earlier):
    return list(lax.optimization_barrier((*arrays, earlier))[:-1])


def swap(piece):
    return lax.ppermute(piece, "core", [(0, 1), (1, 0)])


def per_device(
    nf,
    nx,
    hidden,
    queries,
    cache_keys,
    cache_values,
    new_values,
    lengths,
    base_weight,
    delta_values,
    delta_scales,
    block_order,
):
    steps, rows, width = hidden.shape
    cols = base_weight.shape[1]
    batches = rows // RB
    count = row_count(steps * batches, nx)
    x = lax.axis_index("tx")
    core = lax.axis_index("core")
    depth = 2 * nx * width // nf
    own = delta_values.shape[0]
    split = 2 if own % BLK == 0 else 1

    def to_shift(d, e):
        return [(s * 2 + c, (s - d) % nx * 2 + (c ^ e)) for s in range(nx) for c in range(2)]

    shifts = [(d, e) for d in range(nx) for e in range(2)]
    sent = []
    for e in range(2):
        to = lax.bitwise_xor(core, e)
        sent.append(
            jnp.stack([part_of(delta_values, (2 * q + to) * cols, cols, 1) for q in range(nx)])
        )
    scales = [delta_scales.astype(jnp.float32)]
    scales += [lax.ppermute(scales[0], "tx", shift_of(nx, d)) for d in range(1, nx)]

    flat = hidden.reshape(steps * rows, width)
    whole_rows = swap(flat)

    def rows_of(array, d):
        start = first_group(lax.rem(x + d, nx), steps * batches, nx) * RB
        return part_of(array, start, count * RB, 0)

    held = [[None] * nx for _ in range(nx)]
    for d in range(1, nx):
        came = lax.ppermute(rows_of(flat, (-d) % nx), "tx", shift_of(nx, d))
        ready = [came]
        for early in (*sent, scales[d]):
            ready = after(ready, early)
        held[d][0] = (came, swap(ready[0]))
    if nx == steps and count * RB == rows:
        pieces = [hidden, whole_rows.reshape(hidden.shape)]
    else:
        pieces = [rows_of(flat, 0), rows_of(whole_rows, 0)]
    pieces += [p for d in range(1, nx) for p in held[d][0]]
    mine = scatter(block_order, pieces, nf, split)

    behind = after(sent, held[-1][0][0])
    ws = [sent[0]]
    for d, e in shifts[1:]:
        ws.append(lax.ppermute((behind if d else sent)[e], ("tx", "core"), to_shift(d, e)))
    arrived = ws[1:]
    if split > 1:
        ws[:2] = scale_rows(scales, shifts[:2], ws[:2])
    if split == 1:
        by_chip = jnp.repeat(jnp.roll(jnp.stack(scales), x, axis=0), BLK, axis=2)
        whole = jnp.zeros((nx, depth, cols), jnp.bfloat16)
        for (d, e), piece in zip(shifts, ws):
            at = (lax.rem(x + d, nx) * 2 + lax.bitwise_xor(core, e)) * own
            factor = jnp.take(by_chip, (at + jnp.arange(own)) // BLK, axis=1)
            piece = (piece.astype(jnp.float32) * factor).astype(jnp.bfloat16)
            whole = lax.dynamic_update_slice_in_dim(whole, piece, at, 1)
        ws = [whole]

    (soon,) = after([flat], mine)
    late = []
    for d in range(1, nx):
        for r in range(1, nx):
            start = first_group(lax.rem(x + (r - d) % nx, nx), steps * batches, nx) * RB
            late.append(part_of(soon, start, count * RB, 0))
            (piece,) = after(late[-1:], arrived[-1])
            came = lax.ppermute(piece, "tx", shift_of(nx, d))
            held[d][r] = (came, swap(came))

    owners = [lax.rem(x + d, nx) * 2 + lax.bitwise_xor(core, e) for d, e in shifts]
    owners = jnp.stack(owners)
    first, then = after([owners, lengths], mine)
    for piece in (*late, *ws[:1]):
        (first,) = after([first], piece)
    early = [held[d][0][e] for d in range(1, nx) for e in range(2)]
    plan = ((0,),) * 2 + ((1,),) * len(early)
    near, far = base_product(first, plan, [flat, whole_rows, *early], base_weight, MIDDLE)
    shape = (steps, batches, RB)
    share = cached(
        then, queries.reshape(shape + queries.shape[2:]), cache_keys, cache_values
    )
    if split > 1:
        for earlier in (near, far, share[0]):
            scales = after(scales, earlier)
        ws[2:] = scale_rows(scales, shifts[:1:-1], ws[:1:-1])[::-1]
    mine = lax.all_to_all(mine, "fsdp", 0, 0, tiled=True)
    xs = [mine.reshape(nf * count * RB, depth // split)]
    for earlier in (*arrived[:1], *ws[-2:], near, far, share[0]):
        xs = after(xs, earlier)
    if split > 1:
        xs.append(swap(xs[0]))
        partial = product(xs[0], ws[0::2], nf, last=False)
        partial = product(xs[1], ws[1::2], nf, partial)
    else:
        partial = product(xs[0], ws, nf)
    parts = lax.all_to_all(
        partial.reshape(nf * nx, count * RB, cols), ("fsdp", "tx"), 0, 0, tiled=True
    ).reshape(nf, nx, count * RB, cols)
    remaining = [held[d][r][e] for d in range(1, nx) for e in range(2) for r in range(1, nx)]
    plan = (tuple(range(nx - 1)),) * (2 * (nx - 1))
    late = base_product(after([owners[2:]], partial)[0], plan, remaining, base_weight, LATE)
    attended, new_keys = merge(parts, near, far, late, *share, new_values.reshape(shape + (cols,)))
    return (attended.reshape(queries.shape), new_keys.reshape(steps, rows, cols))


def solution(mesh):
    nf, nt = mesh.shape["fsdp"], mesh.shape["tp"]
    fine = Mesh(mesh.devices.reshape(nf, nt // 2, 2), ("fsdp", "tx", "core"))
    tp = ("tx", "core")
    in_specs = (
        P(None, "fsdp", tp),
        P(None, "fsdp", tp),
        P("fsdp", None, tp),
        P("fsdp", None, tp),
        P(None, "fsdp", tp),
        P("fsdp"),
        P(None, tp),
        P(("fsdp", "tx", "core"), None),
        P("fsdp", tp),
        P(),
    )
    out_specs = (P(None, "fsdp", tp), P(None, "fsdp", tp))
    return jax.shard_map(
        functools.partial(per_device, nf, nt // 2),
        mesh=fine,
        in_specs=in_specs,
        out_specs=out_specs,
        check_vma=False,
    )
```
